256 devices in a mesh: dp: 16 (over z, y_lo), mp: 16 (over y_hi, x, core).
Axes of the slice: x: 4, y: 4 (y_hi: 2, y_lo: 2; y = y_hi * 2 + y_lo), z: 8, core: 2. Of those that a mesh axis runs over, the one named last changes fastest.
Arguments:
- grad_out: bfloat16 [16, 2048, 4096], P('dp', 'mp'), may hold values from -0.375 to 0.375
- hidden: bfloat16 [16, 2048, 14336], P('dp', None, 'mp'), may hold values from -6 to 6
- error: bfloat16 [16, 14336, 4096], P('dp', 'mp'), may hold values from -18 to 18
- q_prev: bfloat16 [4096, 64], replicated, may hold values from -6 to 6
Outputs:
- p_factor: bfloat16 [14336, 64], P('mp')
- q_factor: bfloat16 [4096, 64], replicated
The draws below stay inside these ranges and needn't reach their ends.
All inputs are finite; a program needn't handle non-finite values.
Results may differ from the reference program's by a relative error of at most 0.005.
Values may be sent and summed in bfloat16 or wider, within the bound.
No kernel may reach another device: no remote copies, remote signals or barrier semaphores. Data moves between devices by JAX's collectives and lax.ppermute only.
A program may use at most 64 MiB of HBM per device.

```python
import jax
import jax.numpy as jnp
from jax import lax

D = 4096
FF = 14336
R = 64
GROUP_TOK = 2048
N_DP = 16


def raised(drawn, rng, source, target, blocks, factor):
    owner, partner = [(jnp.arange(drawn.shape[dim]) // (drawn.shape[dim] // blocks)).reshape([-1 if axis == dim else 1 for axis in range(drawn.ndim)]) for dim in (source, target)]
    chosen = jax.random.permutation(rng, blocks)[partner]
    strong = (owner == chosen) | (owner == (partner + blocks // 2) % blocks)
    return jnp.where(strong, factor * drawn, drawn)


def steps_of(rng, shape, pieces, smallest, largest):
    def one(axis_at, shards_of):
        draws = jax.random.uniform(jax.random.fold_in(jax.random.fold_in(rng, 6), axis_at), (shards_of,), jnp.float32, smallest / len(pieces), largest / len(pieces))
        return jnp.repeat(jnp.exp(draws), shape[axis_at] // shards_of).reshape((-1,) + (1,) * (len(shape) - axis_at - 1))

    gain = one(*pieces[0])
    for cut in pieces[1:]:
        gain = gain * one(*cut)
    return gain


def scatter_about(key, shape, width, limit, split=(), held_as=jnp.bfloat16):
    entries = width * jax.random.normal(key, shape, jnp.float32)
    if split:
        entries = entries * steps_of(key, shape, split, -0.22, 0.18)
    return jnp.clip(entries, -limit, limit).astype(held_as)


def gaussian_with(key, dims, width, limit, split, heavy, held_as=jnp.bfloat16):
    array = width * jax.random.normal(key, dims, jnp.float32)
    if split:
        array = array * steps_of(key, dims, split, -0.22, 0.18)
    return jnp.clip(raised(array, jax.random.fold_in(key, 3), *heavy), -limit, limit).astype(held_as)


def setup_inputs(seed: int = 0) -> dict:
    arg_keys = jax.random.split(jax.random.key(seed), 5)
    grad_out = scatter_about(arg_keys[0], (N_DP, GROUP_TOK, D), (GROUP_TOK // 9) ** -0.5, 0.375, ((0, 16), (1, 16)))
    hidden = scatter_about(arg_keys[1], (N_DP, GROUP_TOK, FF), 1.0, 6.0, ((0, 16), (2, 16)))
    error = gaussian_with(arg_keys[2], (N_DP, FF, D), 3.0, 18.0, ((0, 16), (1, 16)), (1, 2, 16, 2.0))
    q_prev = scatter_about(arg_keys[3], (D, R), 1.0, 6.0)
    return {"grad_out": grad_out, "hidden": hidden, "error": error, "q_prev": q_prev}


def reference(grad_out, hidden, error, q_prev):

    def left_step(total, group):
        g_rows, h_rows, e_rows = group
        proj = jnp.dot(g_rows.astype(jnp.float32), q_prev.astype(jnp.float32), preferred_element_type=jnp.float32).astype(jnp.bfloat16)
        term = jnp.dot(h_rows.T.astype(jnp.float32), proj.astype(jnp.float32), preferred_element_type=jnp.float32)
        term = term + jnp.dot(e_rows.astype(jnp.float32), q_prev.astype(jnp.float32), preferred_element_type=jnp.float32)
        return (total + term, None)
    p_sum, _ = lax.scan(left_step, jnp.zeros((FF, R), jnp.float32), (grad_out, hidden, error))
    gram = jnp.dot(p_sum.T, p_sum, precision=lax.Precision.HIGHEST)
    lower_factor = jnp.linalg.cholesky(gram)
    orth = lax.linalg.triangular_solve(lower_factor, p_sum, left_side=False, lower=True, transpose_a=True)
    orth_b = orth.astype(jnp.bfloat16)

    def right_step(total, group):
        g_rows, h_rows, e_rows = group
        mixed = jnp.dot(h_rows.astype(jnp.float32), orth_b.astype(jnp.float32), preferred_element_type=jnp.float32).astype(jnp.bfloat16)
        term = jnp.dot(g_rows.T.astype(jnp.float32), mixed.astype(jnp.float32), preferred_element_type=jnp.float32)
        term = term + jnp.dot(e_rows.T.astype(jnp.float32), orth_b.astype(jnp.float32), preferred_element_type=jnp.float32)
        return (total + term, None)
    q_sum, _ = lax.scan(right_step, jnp.zeros((D, R), jnp.float32), (grad_out, hidden, error))
    q_factor = (q_sum / N_DP).astype(jnp.bfloat16)
    p_factor = (orth * FF ** 0.5).astype(jnp.bfloat16)
    return (p_factor, q_factor)
```

```python
import math

import jax
import jax.numpy as jnp
from jax import lax
from jax.experimental import pallas as pl
from jax.experimental.pallas import tpu as pltpu
from jax.sharding import Mesh
from jax.sharding import PartitionSpec as P

FF = 14336
AXES = ("z", "ylo", "yhi", "x", "core")
SIZES = (-1, 2, 2, 4, 2)
DP = ("z", "ylo")
MP = ("yhi", "x", "core")
PLANE = ("ylo", "yhi", "x")


def contract(left, right, dims):
    return lax.dot_general(left, right, (dims, ((), ())), preferred_element_type=jnp.float32)


def exchange(parts, axis):
    return lax.all_to_all(parts, axis, split_axis=0, concat_axis=0, tiled=True)


def spread(block, axis):
    size = lax.axis_size(axis)
    return exchange(jnp.broadcast_to(block[None], (size,) + block.shape), axis)


def swap(block):
    return lax.ppermute(block, "core", [(0, 1), (1, 0)])


def total(parts):
    return jnp.sum(parts.astype(jnp.float32), axis=0)


def halves(array):
    high = lax.reduce_precision(array, 8, 7)
    return high.astype(jnp.bfloat16), (array - high).astype(jnp.bfloat16)


def whole(pair):
    width = pair.shape[1] // 2
    return pair[:, :width] + pair[:, width:]


def by_lanes(array, count):
    return array.reshape(array.shape[0], count, -1).transpose(1, 0, 2)


def eliminate(parts_ref, inverse_ref, pair_ref):
    rank = inverse_ref.shape[0]
    gram = [parts_ref[j][rank:].astype(jnp.float32) for j in range(rank // 8)]
    gram = jnp.concatenate(gram, axis=0)
    gram = gram[:, :rank] + gram[:, rank:]
    row_at = lax.broadcasted_iota(jnp.int32, gram.shape, 0)
    column_at = lax.broadcasted_iota(jnp.int32, gram.shape, 1)
    start = jnp.concatenate([gram, (row_at == column_at).astype(jnp.float32)], axis=1)
    rows = [start[8 * b : 8 * b + 8, :] for b in range(rank // 8)]
    place = lax.broadcasted_iota(jnp.int32, (8, 1), 0)
    for k in range(0, rank, 2):
        at, inner = divmod(k, 8)
        one, two = rows[at][inner : inner + 1, :], rows[at][inner + 1 : inner + 2, :]
        pivot = jnp.broadcast_to(one[:, k : k + 1], one.shape)
        beside = jnp.broadcast_to(one[:, k + 1 : k + 2], one.shape)
        below = jnp.broadcast_to(two[:, k + 1 : k + 2], one.shape)
        scale = lax.rsqrt(pivot)
        inverse_ref[k : k + 1, :] = (one * scale)[:, rank:]
        unit = scale * scale
        ratio = beside * unit
        two = two - ratio * one
        scale = lax.rsqrt(below - ratio * beside)
        inverse_ref[k + 1 : k + 2, :] = (two * scale)[:, rank:]
        two = two * (scale * scale)
        one = one * unit - ratio * two
        for b in range(at, rank // 8):
            left = rows[b] - rows[b][:, k : k + 1] * one - rows[b][:, k + 1 : k + 2] * two
            rows[b] = jnp.where(place > inner + 1, left, rows[b]) if b == at else left
    inverse = inverse_ref[...] * math.sqrt(FF)
    high = inverse.astype(jnp.bfloat16)
    low = inverse - high.astype(jnp.float32)
    pair_ref[...] = jnp.concatenate([high, low.astype(jnp.bfloat16)], axis=1)


def inverse_factor(parts, rank):
    return pl.pallas_call(
        eliminate,
        out_shape=[
            jax.ShapeDtypeStruct((rank, rank), jnp.float32),
            jax.ShapeDtypeStruct((rank, 2 * rank), jnp.bfloat16),
        ],
        in_specs=[pl.BlockSpec(memory_space=pltpu.VMEM)],
        out_specs=[pl.BlockSpec(memory_space=pltpu.VMEM)] * 2,
        cost_estimate=pl.CostEstimate(flops=4_000_000_000, bytes_accessed=49152, transcendentals=64),
        name="inverse_factor",
    )(parts)


def on_device(grad_out, hidden, error, q_prev):
    bf16, f32 = jnp.bfloat16, jnp.float32
    g_rows, h_rows, e_rows = grad_out[0], hidden[0], error[0]
    groups, parts, plane = lax.axis_size(DP), lax.axis_size(MP), lax.axis_size(PLANE)
    rank = q_prev.shape[1]
    units = h_rows.shape[1]
    some = rank // parts

    proj_local = jnp.dot(g_rows, q_prev, preferred_element_type=f32).astype(bf16)
    first, proj_local = lax.optimization_barrier((lax.axis_index("core") == 0, proj_local))
    proj = spread(proj_local, MP).reshape(h_rows.shape[0], rank)
    base = jnp.dot(e_rows, q_prev, preferred_element_type=f32)
    p_local = base + contract(h_rows, proj, ((0,), (0,)))
    p_terms = p_local.astype(bf16).reshape(groups, units // groups, rank)
    p_part = total(exchange(p_terms, DP)).astype(bf16)
    p_sum = spread(p_part, DP).reshape(units, rank)

    gram_terms = jnp.concatenate(halves(contract(p_sum, p_sum, ((0,), (0,)))), axis=1)
    gram_terms = jnp.pad(gram_terms.reshape(parts, some, -1), ((0, 0), (0, 8 - some), (0, 0)))
    mixed_terms = by_lanes(contract(p_sum, h_rows, ((0,), (1,))).astype(bf16), parts)
    got = exchange(jnp.concatenate([mixed_terms, gram_terms], axis=1), MP)
    mixed = total(got[:, :rank]).astype(bf16)
    gram_rows = jnp.concatenate(halves(whole(total(got[:, rank : rank + some]))), axis=1)

    q_local = contract(p_sum, e_rows, ((0,), (0,))) + contract(mixed, g_rows, ((1,), (0,)))
    half = q_local.shape[1] // 2
    left, right = q_local[:, :half], q_local[:, half:]
    other = swap(jnp.where(first, right, left).astype(bf16))
    other_rows = swap(gram_rows)
    gram_rows = jnp.concatenate(
        [jnp.where(first, gram_rows, other_rows), jnp.where(first, other_rows, gram_rows)]
    )
    q_pair = (jnp.where(first, left, right) + other.astype(f32)).astype(bf16)
    gram_rows = jnp.broadcast_to(gram_rows[None], (plane,) + gram_rows.shape)
    got = exchange(jnp.concatenate([by_lanes(q_pair, plane), gram_rows], axis=1), PLANE)
    q_share = total(got[:, :rank]).astype(bf16)
    q_share, got = lax.optimization_barrier((q_share, got))
    inverse, pair = inverse_factor(got, rank)
    q_share = total(spread(q_share, "z"))
    q_share = jnp.dot(inverse / groups, q_share, precision=lax.Precision.HIGHEST).astype(bf16)
    mine = spread(q_share, PLANE).transpose(1, 0, 2).reshape(rank, -1)
    other = swap(mine)
    q_factor = jnp.concatenate(
        [jnp.where(first, mine, other), jnp.where(first, other, mine)], axis=1
    ).T
    twice = jnp.concatenate([p_sum, p_sum], axis=1)
    p_factor = contract(twice, pair, ((1,), (1,))).astype(bf16)
    return (p_factor, q_factor)


def solution(mesh):
    by_chip = Mesh(mesh.devices.reshape(SIZES), AXES)
    placed = (P(DP, MP, None), P(DP, None, MP), P(DP, MP, None), P())
    return jax.shard_map(
        on_device, mesh=by_chip, in_specs=placed, out_specs=(P(MP, None), P()), check_vma=False
    )
```

```python
import math

import jax
import jax.numpy as jnp
from jax import lax
from jax.experimental import pallas as pl
from jax.experimental.pallas import tpu as pltpu
from jax.sharding import Mesh
from jax.sharding import PartitionSpec as P

FF = 14336
GROUPS = 16
VMEM_BYTES = 4 << 20
AXES = ("z", "ylo", "yhi", "x", "core")
SIZES = (-1, 2, 2, 4, 2)
DP = ("z", "ylo")
MP = ("yhi", "x", "core")
PLANE = ("ylo", "yhi", "x")


def contract(left, right, dims):
    return lax.dot_general(left, right, (dims, ((), ())), preferred_element_type=jnp.float32)


def exchange(parts, axis):
    return lax.all_to_all(parts, axis, split_axis=0, concat_axis=0, tiled=True)


def spread(block, axis):
    size = lax.axis_size(axis)
    return exchange(jnp.broadcast_to(block[None], (size,) + block.shape), axis)


def swap(block):
    return lax.ppermute(block, "core", [(0, 1), (1, 0)])


def total(parts):
    return jnp.sum(parts.astype(jnp.float32), axis=0)


def halves(array):
    high = lax.reduce_precision(array, 8, 7)
    return high.astype(jnp.bfloat16), (array - high).astype(jnp.bfloat16)


def whole(pair):
    width = pair.shape[1] // 2
    return pair[:, :width] + pair[:, width:]


def by_lanes(array, count):
    return array.reshape(array.shape[0], count, -1).transpose(1, 0, 2)


def eliminate(zero_ref, one_ref, q_pair_ref, p_pair_ref, inverse_ref):
    rank = inverse_ref.shape[0]
    gram = []
    for j in range(rank // 8):
        gram += [ref[j].astype(jnp.float32)[:4] for ref in (zero_ref, one_ref)]
    gram = jnp.concatenate(gram, axis=0)
    gram = gram[:, :rank] + gram[:, rank:]
    row_at = lax.broadcasted_iota(jnp.int32, gram.shape, 0)
    column_at = lax.broadcasted_iota(jnp.int32, gram.shape, 1)
    start = jnp.concatenate([gram, (row_at == column_at).astype(jnp.float32)], axis=1)
    rows = [start[8 * b : 8 * b + 8, :] for b in range(rank // 8)]
    place = lax.broadcasted_iota(jnp.int32, (8, 1), 0)
    for k in range(0, rank, 2):
        at, inner = divmod(k, 8)
        one, two = rows[at][inner : inner + 1, :], rows[at][inner + 1 : inner + 2, :]
        pivot = jnp.broadcast_to(one[:, k : k + 1], one.shape)
        beside = jnp.broadcast_to(one[:, k + 1 : k + 2], one.shape)
        below = jnp.broadcast_to(two[:, k + 1 : k + 2], one.shape)
        scale = lax.rsqrt(pivot)
        inverse_ref[k : k + 1, :] = (one * scale)[:, rank:]
        unit = scale * scale
        ratio = beside * unit
        two = two - ratio * one
        scale = lax.rsqrt(below - ratio * beside)
        inverse_ref[k + 1 : k + 2, :] = (two * scale)[:, rank:]
        two = two * (scale * scale)
        one = one * unit - ratio * two
        for b in range(at, rank // 8):
            left = rows[b] - rows[b][:, k : k + 1] * one - rows[b][:, k + 1 : k + 2] * two
            rows[b] = jnp.where(place > inner + 1, left, rows[b]) if b == at else left
    inverse = inverse_ref[...]
    q_pair_ref[...] = halves_in(inverse * (1.0 / GROUPS))
    p_pair_ref[...] = halves_in(inverse * math.sqrt(FF))


def halves_in(array):
    high = array.astype(jnp.bfloat16)
    low = (array - high.astype(jnp.float32)).astype(jnp.bfloat16)
    return jnp.concatenate([high, low], axis=1)


def inverse_factor(zero, one, rank):
    pair = jax.ShapeDtypeStruct((rank, 2 * rank), jnp.bfloat16)
    return pl.pallas_call(
        eliminate,
        out_shape=[pair, pair],
        in_specs=[pl.BlockSpec(memory_space=pltpu.VMEM)] * 2,
        out_specs=[pl.BlockSpec(memory_space=pltpu.VMEM)] * 2,
        scratch_shapes=[pltpu.VMEM((rank, rank), jnp.float32)],
        cost_estimate=pl.CostEstimate(flops=4_000_000_000, bytes_accessed=49152, transcendentals=64),
        compiler_params=pltpu.CompilerParams(vmem_limit_bytes=VMEM_BYTES),
        name="inverse_factor",
    )(zero, one)


def scale_share(parts_ref, pair_ref, out_ref):
    rank = pair_ref.shape[0]
    share = parts_ref[0].astype(jnp.float32)
    for j in range(1, parts_ref.shape[0]):
        share = share + parts_ref[j].astype(jnp.float32)
    high = share.astype(jnp.bfloat16)
    low = (share - high.astype(jnp.float32)).astype(jnp.bfloat16)
    pair = pair_ref[...]
    scaled = contract(pair, jnp.concatenate([high, high], axis=0), ((1,), (0,)))
    scaled = scaled + contract(pair[:, :rank], low, ((1,), (0,)))
    scaled = scaled.astype(jnp.bfloat16)
    for j in range(out_ref.shape[0]):
        out_ref[j] = scaled


def scaled_copies(parts, pair, count):
    return pl.pallas_call(
        scale_share,
        out_shape=jax.ShapeDtypeStruct((count,) + parts.shape[1:], jnp.bfloat16),
        in_specs=[pl.BlockSpec(memory_space=pltpu.VMEM)] * 2,
        out_specs=pl.BlockSpec(memory_space=pltpu.VMEM),
        cost_estimate=pl.CostEstimate(flops=4_000_000, bytes_accessed=409600, transcendentals=0),
        compiler_params=pltpu.CompilerParams(vmem_limit_bytes=VMEM_BYTES),
        name="scaled_copies",
    )(parts, pair)


def on_device(grad_out, hidden, error, q_prev):
    bf16, f32 = jnp.bfloat16, jnp.float32
    g_rows, h_rows, e_rows = grad_out[0], hidden[0], error[0]
    groups, parts, plane = lax.axis_size(DP), lax.axis_size(MP), lax.axis_size(PLANE)
    rank = q_prev.shape[1]
    units = h_rows.shape[1]
    some = rank // parts

    proj_local = jnp.dot(g_rows, q_prev, preferred_element_type=f32).astype(bf16)
    first, proj_local = lax.optimization_barrier((lax.axis_index("core") == 0, proj_local))
    proj = spread(proj_local, MP).reshape(h_rows.shape[0], rank)
    base = jnp.dot(e_rows, q_prev, preferred_element_type=f32)
    p_local = base + contract(h_rows, proj, ((0,), (0,)))
    p_terms = p_local.astype(bf16).reshape(groups, units // groups, rank)
    p_part = total(exchange(p_terms, DP)).astype(bf16)
    p_sum = spread(p_part, DP).reshape(units, rank)

    gram_terms = jnp.concatenate(halves(contract(p_sum, p_sum, ((0,), (0,)))), axis=1)
    gram_terms = jnp.pad(gram_terms.reshape(parts, some, -1), ((0, 0), (0, 8 - some), (0, 0)))
    mixed_terms = by_lanes(contract(p_sum, h_rows, ((0,), (1,))).astype(bf16), parts)
    got = exchange(jnp.concatenate([mixed_terms, gram_terms], axis=1), MP)
    mixed = total(got[:, :rank]).astype(bf16)
    gram_rows = jnp.concatenate(halves(whole(total(got[:, rank : rank + some]))), axis=1)

    q_local = contract(p_sum, e_rows, ((0,), (0,))) + contract(mixed, g_rows, ((1,), (0,)))
    half = q_local.shape[1] // 2
    left, right = q_local[:, :half], q_local[:, half:]
    other = swap(jnp.where(first, right, left).astype(bf16))
    gram_rows = jnp.pad(gram_rows, ((0, 8 - some), (0, 0)))
    q_pair = (jnp.where(first, left, right) + other.astype(f32)).astype(bf16)
    gram_rows = jnp.broadcast_to(gram_rows[None], (plane,) + gram_rows.shape)
    got = exchange(jnp.concatenate([by_lanes(q_pair, plane), gram_rows], axis=1), PLANE)
    q_share = total(got[:, :rank]).astype(bf16)
    q_share, got = lax.optimization_barrier((q_share, got))
    own_rows = got[: plane // 2, rank:]
    other_rows = swap(own_rows)
    zero_rows = jnp.where(first, own_rows, other_rows)
    one_rows = jnp.where(first, other_rows, own_rows)
    q_factors, p_factors = inverse_factor(zero_rows, one_rows, rank)
    q_copies = scaled_copies(spread(q_share, "z"), q_factors, plane)
    mine = exchange(q_copies, PLANE).transpose(1, 0, 2).reshape(rank, -1)
    other = swap(mine)
    q_factor = jnp.concatenate(
        [jnp.where(first, mine, other), jnp.where(first, other, mine)], axis=1
    ).T
    twice = jnp.concatenate([p_sum, p_sum], axis=1)
    p_factor = contract(twice, p_factors, ((1,), (1,))).astype(bf16)
    return (p_factor, q_factor)


def solution(mesh):
    by_chip = Mesh(mesh.devices.reshape(SIZES), AXES)
    placed = (P(DP, MP, None), P(DP, None, MP), P(DP, MP, None), P())
    return jax.shard_map(
        on_device, mesh=by_chip, in_specs=placed, out_specs=(P(MP, None), P()), check_vma=False
    )
```

```python
import math

import jax
import jax.numpy as jnp
from jax import lax
from jax.experimental import pallas as pl
from jax.experimental.pallas import tpu as pltpu
from jax.sharding import Mesh
from jax.sharding import PartitionSpec as P

FF = 14336
GROUPS = 16
VMEM_BYTES = 4 << 20
ROWS, LANES = 32, 128
AXES = ("z", "ylo", "yhi", "x", "core")
SIZES = (-1, 2, 2, 4, 2)
DP = ("z", "ylo")
MP = ("yhi", "x", "core")
PLANE = ("ylo", "yhi", "x")


def contract(left, right, dims):
    return lax.dot_general(left, right, (dims, ((), ())), preferred_element_type=jnp.float32)


def exchange(parts, axis):
    return lax.all_to_all(parts, axis, split_axis=0, concat_axis=0, tiled=True)


def spread(block, axis):
    size = lax.axis_size(axis)
    return exchange(jnp.broadcast_to(block[None], (size,) + block.shape), axis)


def swap(block):
    return lax.ppermute(block, "core", [(0, 1), (1, 0)])


def total(parts):
    return jnp.sum(parts.astype(jnp.float32), axis=0)


def halves(array):
    high = lax.reduce_precision(array, 8, 7)
    return high.astype(jnp.bfloat16), (array - high).astype(jnp.bfloat16)


def whole(pair):
    width = pair.shape[1] // 2
    return pair[:, :width] + pair[:, width:]


def by_lanes(array, count):
    return array.reshape(array.shape[0], count, -1).transpose(1, 0, 2)


def places(units):
    return [(r, c) for r in (0, ROWS) for c in range(0, units, LANES)]


def left_kernel(proj_ref, h_ref, base_ref, out_ref):
    proj = jnp.concatenate([proj_ref[j] for j in range(proj_ref.shape[0])], axis=1)
    terms = base_ref[...] + contract(proj, h_ref[...], ((1,), (0,)))
    terms = terms.astype(jnp.bfloat16)
    used = places(terms.shape[1])
    for j, (r, c) in enumerate(used):
        out_ref[j] = terms[r : r + ROWS, c : c + LANES]
    for j in range(len(used), out_ref.shape[0]):
        out_ref[j] = jnp.zeros((ROWS, LANES), jnp.bfloat16)


def left_terms(proj, h_rows, base, count):
    return pl.pallas_call(
        left_kernel,
        out_shape=jax.ShapeDtypeStruct((count, ROWS, LANES), jnp.bfloat16),
        in_specs=[pl.BlockSpec(memory_space=pltpu.VMEM)] * 3,
        out_specs=pl.BlockSpec(memory_space=pltpu.VMEM),
        cost_estimate=pl.CostEstimate(flops=1_000_000_000, bytes_accessed=4 << 20, transcendentals=0),
        compiler_params=pltpu.CompilerParams(vmem_limit_bytes=3 * VMEM_BYTES),
        name="left_terms",
    )(proj, h_rows, base)


def mix_kernel(parts_ref, h_ref, out_ref, p_ref):
    for j, (r, c) in enumerate(places(p_ref.shape[1])):
        p_ref[r : r + ROWS, c : c + LANES] = parts_ref[j]
    p = p_ref[...]
    gram = contract(p, p, ((1,), (1,)))
    high = gram.astype(jnp.bfloat16).astype(jnp.float32)
    pair = jnp.concatenate([high, gram - high], axis=1)
    mixed = contract(p, h_ref[...], ((1,), (1,))).astype(jnp.bfloat16)
    count = out_ref.shape[0]
    some = pair.shape[0] // count
    fill = jnp.zeros((8 - some, LANES), jnp.float32)
    for j in range(count):
        rows = jnp.concatenate([pair[some * j : some * (j + 1)], fill], axis=0)
        block = mixed[:, j * LANES : (j + 1) * LANES]
        out_ref[j] = jnp.concatenate([block, rows.astype(jnp.bfloat16)], axis=0)


def mixed_terms(parts, h_rows, rank, units, count):
    return pl.pallas_call(
        mix_kernel,
        out_shape=[
            jax.ShapeDtypeStruct((count, rank + 8, LANES), jnp.bfloat16),
            jax.ShapeDtypeStruct((rank, units), jnp.bfloat16),
        ],
        in_specs=[pl.BlockSpec(memory_space=pltpu.VMEM)] * 2,
        out_specs=[pl.BlockSpec(memory_space=pltpu.VMEM)] * 2,
        cost_estimate=pl.CostEstimate(flops=1_000_000_000, bytes_accessed=4 << 20, transcendentals=0),
        compiler_params=pltpu.CompilerParams(vmem_limit_bytes=3 * VMEM_BYTES),
        name="mixed_terms",
    )(parts, h_rows)


def eliminate(zero_ref, one_ref, q_pair_ref, p_pair_ref, inverse_ref):
    rank = inverse_ref.shape[0]
    gram = []
    for j in range(rank // 8):
        gram += [ref[j].astype(jnp.float32)[:4] for ref in (zero_ref, one_ref)]
    gram = jnp.concatenate(gram, axis=0)
    gram = gram[:, :rank] + gram[:, rank:]
    row_at = lax.broadcasted_iota(jnp.int32, gram.shape, 0)
    column_at = lax.broadcasted_iota(jnp.int32, gram.shape, 1)
    start = jnp.concatenate([gram, (row_at == column_at).astype(jnp.float32)], axis=1)
    rows = [start[8 * b : 8 * b + 8, :] for b in range(rank // 8)]
    place = lax.broadcasted_iota(jnp.int32, (8, 1), 0)
    for k in range(0, rank, 2):
        at, inner = divmod(k, 8)
        one, two = rows[at][inner : inner + 1, :], rows[at][inner + 1 : inner + 2, :]
        pivot = jnp.broadcast_to(one[:, k : k + 1], one.shape)
        beside = jnp.broadcast_to(one[:, k + 1 : k + 2], one.shape)
        below = jnp.broadcast_to(two[:, k + 1 : k + 2], one.shape)
        scale = lax.rsqrt(pivot)
        inverse_ref[k : k + 1, :] = (one * scale)[:, rank:]
        unit = scale * scale
        ratio = beside * unit
        two = two - ratio * one
        scale = lax.rsqrt(below - ratio * beside)
        inverse_ref[k + 1 : k + 2, :] = (two * scale)[:, rank:]
        two = two * (scale * scale)
        one = one * unit - ratio * two
        for b in range(at, rank // 8):
            left = rows[b] - rows[b][:, k : k + 1] * one - rows[b][:, k + 1 : k + 2] * two
            rows[b] = jnp.where(place > inner + 1, left, rows[b]) if b == at else left
    inverse = inverse_ref[...]
    q_pair_ref[...] = halves_in(inverse * (1.0 / GROUPS))
    p_pair_ref[...] = halves_in(inverse * math.sqrt(FF))


def halves_in(array):
    high = array.astype(jnp.bfloat16)
    low = (array - high.astype(jnp.float32)).astype(jnp.bfloat16)
    return jnp.concatenate([high, low], axis=1)


def inverse_factor(zero, one, rank):
    pair = jax.ShapeDtypeStruct((rank, 2 * rank), jnp.bfloat16)
    return pl.pallas_call(
        eliminate,
        out_shape=[pair, pair],
        in_specs=[pl.BlockSpec(memory_space=pltpu.VMEM)] * 2,
        out_specs=[pl.BlockSpec(memory_space=pltpu.VMEM)] * 2,
        scratch_shapes=[pltpu.VMEM((rank, rank), jnp.float32)],
        cost_estimate=pl.CostEstimate(flops=4_000_000_000, bytes_accessed=49152, transcendentals=64),
        compiler_params=pltpu.CompilerParams(vmem_limit_bytes=VMEM_BYTES),
        name="inverse_factor",
    )(zero, one)


def scale_share(parts_ref, pair_ref, out_ref):
    rank = pair_ref.shape[0]
    share = parts_ref[0].astype(jnp.float32)
    for j in range(1, parts_ref.shape[0]):
        share = share + parts_ref[j].astype(jnp.float32)
    high = share.astype(jnp.bfloat16)
    low = (share - high.astype(jnp.float32)).astype(jnp.bfloat16)
    pair = pair_ref[...]
    scaled = contract(pair, jnp.concatenate([high, high], axis=0), ((1,), (0,)))
    scaled = scaled + contract(pair[:, :rank], low, ((1,), (0,)))
    scaled = scaled.astype(jnp.bfloat16)
    for j in range(out_ref.shape[0]):
        out_ref[j] = scaled


def scaled_copies(parts, pair, count):
    return pl.pallas_call(
        scale_share,
        out_shape=jax.ShapeDtypeStruct((count,) + parts.shape[1:], jnp.bfloat16),
        in_specs=[pl.BlockSpec(memory_space=pltpu.VMEM)] * 2,
        out_specs=pl.BlockSpec(memory_space=pltpu.VMEM),
        cost_estimate=pl.CostEstimate(flops=4_000_000, bytes_accessed=409600, transcendentals=0),
        compiler_params=pltpu.CompilerParams(vmem_limit_bytes=VMEM_BYTES),
        name="scaled_copies",
    )(parts, pair)


def on_device(grad_out, hidden, error, q_prev):
    bf16, f32 = jnp.bfloat16, jnp.float32
    g_rows, h_rows, e_rows = grad_out[0], hidden[0], error[0]
    groups, parts, plane = lax.axis_size(DP), lax.axis_size(MP), lax.axis_size(PLANE)
    rank = q_prev.shape[1]
    units = h_rows.shape[1]
    some = rank // parts

    proj_local = jnp.dot(g_rows, q_prev, preferred_element_type=f32).astype(bf16)
    first, proj_local = lax.optimization_barrier((lax.axis_index("core") == 0, proj_local))
    proj = spread(proj_local.T, MP)
    base = jnp.dot(e_rows, q_prev, preferred_element_type=f32).T
    p_terms = left_terms(proj, h_rows, base, groups)
    p_part = total(exchange(p_terms, DP)).astype(bf16)
    parts_of_mixed, p_sum = mixed_terms(spread(p_part, DP), h_rows, rank, units, parts)
    got = exchange(parts_of_mixed, MP)
    mixed = total(got[:, :rank]).astype(bf16)
    gram_rows = jnp.concatenate(halves(whole(total(got[:, rank : rank + some]))), axis=1)

    q_local = contract(p_sum, e_rows, ((1,), (0,))) + contract(mixed, g_rows, ((1,), (0,)))
    half = q_local.shape[1] // 2
    left, right = q_local[:, :half], q_local[:, half:]
    other = swap(jnp.where(first, right, left).astype(bf16))
    gram_rows = jnp.pad(gram_rows, ((0, 8 - some), (0, 0)))
    q_pair = (jnp.where(first, left, right) + other.astype(f32)).astype(bf16)
    gram_rows = jnp.broadcast_to(gram_rows[None], (plane,) + gram_rows.shape)
    got = exchange(jnp.concatenate([by_lanes(q_pair, plane), gram_rows], axis=1), PLANE)
    q_share = total(got[:, :rank]).astype(bf16)
    q_share, got = lax.optimization_barrier((q_share, got))
    own_rows = got[: plane // 2, rank:]
    other_rows = swap(own_rows)
    zero_rows = jnp.where(first, own_rows, other_rows)
    one_rows = jnp.where(first, other_rows, own_rows)
    q_factors, p_factors = inverse_factor(zero_rows, one_rows, rank)
    q_copies = scaled_copies(spread(q_share, "z"), q_factors, plane)
    mine = exchange(q_copies, PLANE).transpose(1, 0, 2).reshape(rank, -1)
    other = swap(mine)
    q_factor = jnp.concatenate(
        [jnp.where(first, mine, other), jnp.where(first, other, mine)], axis=1
    ).T
    twice = jnp.concatenate([p_sum, p_sum], axis=0)
    p_factor = contract(p_factors, twice, ((1,), (0,))).astype(bf16).T
    return (p_factor, q_factor)


def solution(mesh):
    by_chip = Mesh(mesh.devices.reshape(SIZES), AXES)
    placed = (P(DP, MP, None), P(DP, None, MP), P(DP, MP, None), P())
    return jax.shard_map(
        on_device, mesh=by_chip, in_specs=placed, out_specs=(P(MP, None), P()), check_vma=False
    )
```

```python
import math

import jax
import jax.numpy as jnp
from jax import lax
from jax.experimental import pallas as pl
from jax.experimental.pallas import tpu as pltpu
from jax.sharding import Mesh
from jax.sharding import PartitionSpec as P

FF = 14336
GROUPS = 16
VMEM_BYTES = 4 << 20
ROWS, LANES = 32, 128
AXES = ("z", "ylo", "yhi", "x", "core")
SIZES = (-1, 2, 2, 4, 2)
DP = ("z", "ylo")
MP = ("yhi", "x", "core")
PLANE = ("ylo", "yhi", "x")


def contract(left, right, dims):
    return lax.dot_general(left, right, (dims, ((), ())), preferred_element_type=jnp.float32)


def exchange(parts, axis):
    return lax.all_to_all(parts, axis, split_axis=0, concat_axis=0, tiled=True)


def spread(block, axis):
    size = lax.axis_size(axis)
    return exchange(jnp.broadcast_to(block[None], (size,) + block.shape), axis)


def swap(block):
    return lax.ppermute(block, "core", [(0, 1), (1, 0)])


def total(parts):
    return jnp.sum(parts.astype(jnp.float32), axis=0)


def halves(array):
    high = lax.reduce_precision(array, 8, 7)
    return high.astype(jnp.bfloat16), (array - high).astype(jnp.bfloat16)


def whole(pair):
    width = pair.shape[1] // 2
    return pair[:, :width] + pair[:, width:]


def by_lanes(array, count):
    return array.reshape(array.shape[0], count, -1).transpose(1, 0, 2)


def small_call(kernel, outs, *operands, spaces=None, scratch=(), name):
    spaces = spaces or [pltpu.VMEM] * len(operands)
    return pl.pallas_call(
        kernel,
        out_shape=[jax.ShapeDtypeStruct(shape, dtype) for shape, dtype in outs],
        in_specs=[pl.BlockSpec(memory_space=space) for space in spaces],
        out_specs=[pl.BlockSpec(memory_space=pltpu.VMEM)] * len(outs),
        scratch_shapes=scratch,
        cost_estimate=pl.CostEstimate(flops=1_000_000_000, bytes_accessed=4 << 20, transcendentals=0),
        compiler_params=pltpu.CompilerParams(vmem_limit_bytes=3 * VMEM_BYTES),
        name=name,
    )(*operands)


def project_kernel(q_ref, g_ref, out_ref):
    proj = contract(q_ref[...], g_ref[...], ((1,), (1,))).astype(jnp.bfloat16)
    for j in range(out_ref.shape[0]):
        out_ref[j] = proj


def base_kernel(q_ref, e_ref, out_ref, held_ref, arrived):
    slots = held_ref.shape[0]
    count = e_ref.shape[0] // LANES

    def fetch(j):
        rows = e_ref.at[pl.ds(j * LANES, LANES)]
        return pltpu.make_async_copy(rows, held_ref.at[j % slots], arrived.at[j % slots])

    for j in range(slots - 1):
        fetch(j).start()
    for j in range(count):
        if j + slots - 1 < count:
            fetch(j + slots - 1).start()
        fetch(j).wait()
        out_ref[:, j * LANES : (j + 1) * LANES] = contract(
            q_ref[...], held_ref[j % slots], ((1,), (1,))
        )


def sum_kernel(parts_ref, out_ref):
    share = parts_ref[0].astype(jnp.float32)
    for j in range(1, parts_ref.shape[0]):
        share = share + parts_ref[j].astype(jnp.float32)
    share = share.astype(jnp.bfloat16)
    for j in range(out_ref.shape[0]):
        out_ref[j] = share


def places(units):
    return [(r, c) for r in (0, ROWS) for c in range(0, units, LANES)]


def left_kernel(proj_ref, h_ref, base_ref, out_ref):
    proj = jnp.concatenate([proj_ref[j] for j in range(proj_ref.shape[0])], axis=1)
    terms = base_ref[...] + contract(proj, h_ref[...], ((1,), (0,)))
    terms = terms.astype(jnp.bfloat16)
    used = places(terms.shape[1])
    for j, (r, c) in enumerate(used):
        out_ref[j] = terms[r : r + ROWS, c : c + LANES]
    for j in range(len(used), out_ref.shape[0]):
        out_ref[j] = jnp.zeros((ROWS, LANES), jnp.bfloat16)


def left_terms(proj, h_rows, base, count):
    return pl.pallas_call(
        left_kernel,
        out_shape=jax.ShapeDtypeStruct((count, ROWS, LANES), jnp.bfloat16),
        in_specs=[pl.BlockSpec(memory_space=pltpu.VMEM)] * 3,
        out_specs=pl.BlockSpec(memory_space=pltpu.VMEM),
        cost_estimate=pl.CostEstimate(flops=1_000_000_000, bytes_accessed=4 << 20, transcendentals=0),
        compiler_params=pltpu.CompilerParams(vmem_limit_bytes=3 * VMEM_BYTES),
        name="left_terms",
    )(proj, h_rows, base)


def mix_kernel(parts_ref, h_ref, out_ref, p_ref):
    for j, (r, c) in enumerate(places(p_ref.shape[1])):
        p_ref[r : r + ROWS, c : c + LANES] = parts_ref[j]
    p = p_ref[...]
    gram = contract(p, p, ((1,), (1,)))
    high = gram.astype(jnp.bfloat16).astype(jnp.float32)
    pair = jnp.concatenate([high, gram - high], axis=1)
    mixed = contract(p, h_ref[...], ((1,), (1,))).astype(jnp.bfloat16)
    count = out_ref.shape[0]
    some = pair.shape[0] // count
    fill = jnp.zeros((8 - some, LANES), jnp.float32)
    for j in range(count):
        rows = jnp.concatenate([pair[some * j : some * (j + 1)], fill], axis=0)
        block = mixed[:, j * LANES : (j + 1) * LANES]
        out_ref[j] = jnp.concatenate([block, rows.astype(jnp.bfloat16)], axis=0)


def mixed_terms(parts, h_rows, rank, units, count):
    return pl.pallas_call(
        mix_kernel,
        out_shape=[
            jax.ShapeDtypeStruct((count, rank + 8, LANES), jnp.bfloat16),
            jax.ShapeDtypeStruct((rank, units), jnp.bfloat16),
        ],
        in_specs=[pl.BlockSpec(memory_space=pltpu.VMEM)] * 2,
        out_specs=[pl.BlockSpec(memory_space=pltpu.VMEM)] * 2,
        cost_estimate=pl.CostEstimate(flops=1_000_000_000, bytes_accessed=4 << 20, transcendentals=0),
        compiler_params=pltpu.CompilerParams(vmem_limit_bytes=3 * VMEM_BYTES),
        name="mixed_terms",
    )(parts, h_rows)


def eliminate(zero_ref, one_ref, q_pair_ref, p_pair_ref, inverse_ref):
    rank = inverse_ref.shape[0]
    gram = []
    for j in range(rank // 8):
        gram += [ref[j].astype(jnp.float32)[:4] for ref in (zero_ref, one_ref)]
    gram = jnp.concatenate(gram, axis=0)
    gram = gram[:, :rank] + gram[:, rank:]
    row_at = lax.broadcasted_iota(jnp.int32, gram.shape, 0)
    column_at = lax.broadcasted_iota(jnp.int32, gram.shape, 1)
    start = jnp.concatenate([gram, (row_at == column_at).astype(jnp.float32)], axis=1)
    rows = [start[8 * b : 8 * b + 8, :] for b in range(rank // 8)]
    place = lax.broadcasted_iota(jnp.int32, (8, 1), 0)
    for k in range(0, rank, 2):
        at, inner = divmod(k, 8)
        one, two = rows[at][inner : inner + 1, :], rows[at][inner + 1 : inner + 2, :]
        pivot = jnp.broadcast_to(one[:, k : k + 1], one.shape)
        beside = jnp.broadcast_to(one[:, k + 1 : k + 2], one.shape)
        below = jnp.broadcast_to(two[:, k + 1 : k + 2], one.shape)
        scale = lax.rsqrt(pivot)
        inverse_ref[k : k + 1, :] = (one * scale)[:, rank:]
        unit = scale * scale
        ratio = beside * unit
        two = two - ratio * one
        scale = lax.rsqrt(below - ratio * beside)
        inverse_ref[k + 1 : k + 2, :] = (two * scale)[:, rank:]
        two = two * (scale * scale)
        one = one * unit - ratio * two
        for b in range(at, rank // 8):
            left = rows[b] - rows[b][:, k : k + 1] * one - rows[b][:, k + 1 : k + 2] * two
            rows[b] = jnp.where(place > inner + 1, left, rows[b]) if b == at else left
    inverse = inverse_ref[...]
    q_pair_ref[...] = halves_in(inverse * (1.0 / GROUPS))
    p_pair_ref[...] = halves_in(inverse * math.sqrt(FF))


def halves_in(array):
    high = array.astype(jnp.bfloat16)
    low = (array - high.astype(jnp.float32)).astype(jnp.bfloat16)
    return jnp.concatenate([high, low], axis=1)


def inverse_factor(zero, one, rank):
    pair = jax.ShapeDtypeStruct((rank, 2 * rank), jnp.bfloat16)
    return pl.pallas_call(
        eliminate,
        out_shape=[pair, pair],
        in_specs=[pl.BlockSpec(memory_space=pltpu.VMEM)] * 2,
        out_specs=[pl.BlockSpec(memory_space=pltpu.VMEM)] * 2,
        scratch_shapes=[pltpu.VMEM((rank, rank), jnp.float32)],
        cost_estimate=pl.CostEstimate(flops=4_000_000_000, bytes_accessed=49152, transcendentals=64),
        compiler_params=pltpu.CompilerParams(vmem_limit_bytes=VMEM_BYTES),
        name="inverse_factor",
    )(zero, one)


def scale_share(parts_ref, pair_ref, out_ref):
    rank = pair_ref.shape[0]
    share = parts_ref[0].astype(jnp.float32)
    for j in range(1, parts_ref.shape[0]):
        share = share + parts_ref[j].astype(jnp.float32)
    high = share.astype(jnp.bfloat16)
    low = (share - high.astype(jnp.float32)).astype(jnp.bfloat16)
    pair = pair_ref[...]
    scaled = contract(pair, jnp.concatenate([high, high], axis=0), ((1,), (0,)))
    scaled = scaled + contract(pair[:, :rank], low, ((1,), (0,)))
    scaled = scaled.astype(jnp.bfloat16)
    for j in range(out_ref.shape[0]):
        out_ref[j] = scaled


def scaled_copies(parts, pair, count):
    return pl.pallas_call(
        scale_share,
        out_shape=jax.ShapeDtypeStruct((count,) + parts.shape[1:], jnp.bfloat16),
        in_specs=[pl.BlockSpec(memory_space=pltpu.VMEM)] * 2,
        out_specs=pl.BlockSpec(memory_space=pltpu.VMEM),
        cost_estimate=pl.CostEstimate(flops=4_000_000, bytes_accessed=409600, transcendentals=0),
        compiler_params=pltpu.CompilerParams(vmem_limit_bytes=VMEM_BYTES),
        name="scaled_copies",
    )(parts, pair)


def on_device(grad_out, hidden, error, q_prev):
    bf16, f32 = jnp.bfloat16, jnp.float32
    g_rows, h_rows, e_rows = grad_out[0], hidden[0], error[0]
    groups, parts, plane = lax.axis_size(DP), lax.axis_size(MP), lax.axis_size(PLANE)
    rank = q_prev.shape[1]
    units = h_rows.shape[1]
    some = rank // parts

    (copies,) = small_call(
        project_kernel, [((parts, rank, LANES), bf16)], q_prev.T, g_rows, name="project"
    )
    first, copies, q_rows = lax.optimization_barrier(
        (lax.axis_index("core") == 0, copies, q_prev.T)
    )
    proj = exchange(copies, MP)
    (base,) = small_call(
        base_kernel,
        [((rank, units), f32)],
        q_rows,
        e_rows,
        spaces=[pltpu.VMEM, pltpu.HBM],
        scratch=[pltpu.VMEM((3, LANES, e_rows.shape[1]), bf16), pltpu.SemaphoreType.DMA((3,))],
        name="base",
    )
    p_terms = left_terms(proj, h_rows, base, groups)
    p_terms = exchange(p_terms, DP)
    (p_copies,) = small_call(sum_kernel, [(p_terms.shape, bf16)], p_terms, name="p_copies")
    parts_of_mixed, p_sum = mixed_terms(exchange(p_copies, DP), h_rows, rank, units, parts)
    got = exchange(parts_of_mixed, MP)
    mixed = total(got[:, :rank]).astype(bf16)
    gram_rows = jnp.concatenate(halves(whole(total(got[:, rank : rank + some]))), axis=1)

    q_local = contract(p_sum, e_rows, ((1,), (0,))) + contract(mixed, g_rows, ((1,), (0,)))
    half = q_local.shape[1] // 2
    left, right = q_local[:, :half], q_local[:, half:]
    other = swap(jnp.where(first, right, left).astype(bf16))
    gram_rows = jnp.pad(gram_rows, ((0, 8 - some), (0, 0)))
    q_pair = (jnp.where(first, left, right) + other.astype(f32)).astype(bf16)
    gram_rows = jnp.broadcast_to(gram_rows[None], (plane,) + gram_rows.shape)
    got = exchange(jnp.concatenate([by_lanes(q_pair, plane), gram_rows], axis=1), PLANE)
    q_share = total(got[:, :rank]).astype(bf16)
    q_share, got = lax.optimization_barrier((q_share, got))
    own_rows = got[: plane // 2, rank:]
    other_rows = swap(own_rows)
    zero_rows = jnp.where(first, own_rows, other_rows)
    one_rows = jnp.where(first, other_rows, own_rows)
    q_factors, p_factors = inverse_factor(zero_rows, one_rows, rank)
    q_copies = scaled_copies(spread(q_share, "z"), q_factors, plane)
    mine = exchange(q_copies, PLANE).transpose(1, 0, 2).reshape(rank, -1)
    other = swap(mine)
    q_factor = jnp.concatenate(
        [jnp.where(first, mine, other), jnp.where(first, other, mine)], axis=1
    ).T
    twice = jnp.concatenate([p_sum, p_sum], axis=0)
    p_factor = contract(p_factors, twice, ((1,), (0,))).astype(bf16).T
    return (p_factor, q_factor)


def solution(mesh):
    by_chip = Mesh(mesh.devices.reshape(SIZES), AXES)
    placed = (P(DP, MP, None), P(DP, None, MP), P(DP, MP, None), P())
    return jax.shard_map(
        on_device, mesh=by_chip, in_specs=placed, out_specs=(P(MP, None), P()), check_vma=False
    )
```

```python
import math

import jax
import jax.numpy as jnp
from jax import lax
from jax.experimental import pallas as pl
from jax.experimental.pallas import tpu as pltpu
from jax.sharding import Mesh
from jax.sharding import PartitionSpec as P

FF = 14336
GROUPS = 16
VMEM_BYTES = 4 << 20
ROWS, LANES = 32, 128
AXES = ("z", "ylo", "yhi", "x", "core")
SIZES = (-1, 2, 2, 4, 2)
DP = ("z", "ylo")
MP = ("yhi", "x", "core")
PLANE = ("ylo", "yhi", "x")


def contract(left, right, dims):
    return lax.dot_general(left, right, (dims, ((), ())), preferred_element_type=jnp.float32)


def exchange(parts, axis):
    return lax.all_to_all(parts, axis, split_axis=0, concat_axis=0, tiled=True)


def spread(block, axis):
    size = lax.axis_size(axis)
    return exchange(jnp.broadcast_to(block[None], (size,) + block.shape), axis)


def swap(block):
    return lax.ppermute(block, "core", [(0, 1), (1, 0)])


def total(parts):
    return jnp.sum(parts.astype(jnp.float32), axis=0)


def halves(array):
    high = lax.reduce_precision(array, 8, 7)
    return high.astype(jnp.bfloat16), (array - high).astype(jnp.bfloat16)


def whole(pair):
    width = pair.shape[1] // 2
    return pair[:, :width] + pair[:, width:]


def by_lanes(array, count):
    return array.reshape(array.shape[0], count, -1).transpose(1, 0, 2)


def sum_kernel(parts_ref, out_ref):
    share = parts_ref[0].astype(jnp.float32)
    for j in range(1, parts_ref.shape[0]):
        share = share + parts_ref[j].astype(jnp.float32)
    share = share.astype(jnp.bfloat16)
    for j in range(out_ref.shape[0]):
        out_ref[j] = share


def sum_copies(parts):
    return pl.pallas_call(
        sum_kernel,
        out_shape=jax.ShapeDtypeStruct(parts.shape, parts.dtype),
        in_specs=[pl.BlockSpec(memory_space=pltpu.VMEM)],
        out_specs=pl.BlockSpec(memory_space=pltpu.VMEM),
        cost_estimate=pl.CostEstimate(flops=65536, bytes_accessed=262144, transcendentals=0),
        compiler_params=pltpu.CompilerParams(vmem_limit_bytes=VMEM_BYTES),
        name="sum_copies",
    )(parts)


def places(units):
    return [(r, c) for r in (0, ROWS) for c in range(0, units, LANES)]


def left_kernel(proj_ref, h_ref, base_ref, out_ref):
    proj = jnp.concatenate([proj_ref[j] for j in range(proj_ref.shape[0])], axis=1)
    terms = base_ref[...] + contract(proj, h_ref[...], ((1,), (0,)))
    terms = terms.astype(jnp.bfloat16)
    used = places(terms.shape[1])
    for j, (r, c) in enumerate(used):
        out_ref[j] = terms[r : r + ROWS, c : c + LANES]
    for j in range(len(used), out_ref.shape[0]):
        out_ref[j] = jnp.zeros((ROWS, LANES), jnp.bfloat16)


def left_terms(proj, h_rows, base, count):
    return pl.pallas_call(
        left_kernel,
        out_shape=jax.ShapeDtypeStruct((count, ROWS, LANES), jnp.bfloat16),
        in_specs=[pl.BlockSpec(memory_space=pltpu.VMEM)] * 3,
        out_specs=pl.BlockSpec(memory_space=pltpu.VMEM),
        cost_estimate=pl.CostEstimate(flops=1_000_000_000, bytes_accessed=4 << 20, transcendentals=0),
        compiler_params=pltpu.CompilerParams(vmem_limit_bytes=3 * VMEM_BYTES),
        name="left_terms",
    )(proj, h_rows, base)


def mix_kernel(parts_ref, h_ref, out_ref, p_ref):
    for j, (r, c) in enumerate(places(p_ref.shape[1])):
        p_ref[r : r + ROWS, c : c + LANES] = parts_ref[j]
    p = p_ref[...]
    gram = contract(p, p, ((1,), (1,)))
    high = gram.astype(jnp.bfloat16).astype(jnp.float32)
    pair = jnp.concatenate([high, gram - high], axis=1)
    mixed = contract(p, h_ref[...], ((1,), (1,))).astype(jnp.bfloat16)
    count = out_ref.shape[0]
    some = pair.shape[0] // count
    fill = jnp.zeros((8 - some, LANES), jnp.float32)
    for j in range(count):
        rows = jnp.concatenate([pair[some * j : some * (j + 1)], fill], axis=0)
        block = mixed[:, j * LANES : (j + 1) * LANES]
        out_ref[j] = jnp.concatenate([block, rows.astype(jnp.bfloat16)], axis=0)


def mixed_terms(parts, h_rows, rank, units, count):
    return pl.pallas_call(
        mix_kernel,
        out_shape=[
            jax.ShapeDtypeStruct((count, rank + 8, LANES), jnp.bfloat16),
            jax.ShapeDtypeStruct((rank, units), jnp.bfloat16),
        ],
        in_specs=[pl.BlockSpec(memory_space=pltpu.VMEM)] * 2,
        out_specs=[pl.BlockSpec(memory_space=pltpu.VMEM)] * 2,
        cost_estimate=pl.CostEstimate(flops=1_000_000_000, bytes_accessed=4 << 20, transcendentals=0),
        compiler_params=pltpu.CompilerParams(vmem_limit_bytes=3 * VMEM_BYTES),
        name="mixed_terms",
    )(parts, h_rows)


def eliminate(zero_ref, one_ref, q_pair_ref, p_pair_ref, inverse_ref):
    rank = inverse_ref.shape[0]
    gram = []
    for j in range(rank // 8):
        gram += [ref[j].astype(jnp.float32)[:4] for ref in (zero_ref, one_ref)]
    gram = jnp.concatenate(gram, axis=0)
    gram = gram[:, :rank] + gram[:, rank:]
    row_at = lax.broadcasted_iota(jnp.int32, gram.shape, 0)
    column_at = lax.broadcasted_iota(jnp.int32, gram.shape, 1)
    start = jnp.concatenate([gram, (row_at == column_at).astype(jnp.float32)], axis=1)
    rows = [start[8 * b : 8 * b + 8, :] for b in range(rank // 8)]
    place = lax.broadcasted_iota(jnp.int32, (8, 1), 0)
    for k in range(0, rank, 2):
        at, inner = divmod(k, 8)
        one, two = rows[at][inner : inner + 1, :], rows[at][inner + 1 : inner + 2, :]
        pivot = jnp.broadcast_to(one[:, k : k + 1], one.shape)
        beside = jnp.broadcast_to(one[:, k + 1 : k + 2], one.shape)
        below = jnp.broadcast_to(two[:, k + 1 : k + 2], one.shape)
        scale = lax.rsqrt(pivot)
        inverse_ref[k : k + 1, :] = (one * scale)[:, rank:]
        unit = scale * scale
        ratio = beside * unit
        two = two - ratio * one
        scale = lax.rsqrt(below - ratio * beside)
        inverse_ref[k + 1 : k + 2, :] = (two * scale)[:, rank:]
        two = two * (scale * scale)
        one = one * unit - ratio * two
        for b in range(at, rank // 8):
            left = rows[b] - rows[b][:, k : k + 1] * one - rows[b][:, k + 1 : k + 2] * two
            rows[b] = jnp.where(place > inner + 1, left, rows[b]) if b == at else left
    inverse = inverse_ref[...]
    q_pair_ref[...] = halves_in(inverse * (1.0 / GROUPS))
    p_pair_ref[...] = halves_in(inverse * math.sqrt(FF))


def halves_in(array):
    high = array.astype(jnp.bfloat16)
    low = (array - high.astype(jnp.float32)).astype(jnp.bfloat16)
    return jnp.concatenate([high, low], axis=1)


def inverse_factor(zero, one, rank):
    pair = jax.ShapeDtypeStruct((rank, 2 * rank), jnp.bfloat16)
    return pl.pallas_call(
        eliminate,
        out_shape=[pair, pair],
        in_specs=[pl.BlockSpec(memory_space=pltpu.VMEM)] * 2,
        out_specs=[pl.BlockSpec(memory_space=pltpu.VMEM)] * 2,
        scratch_shapes=[pltpu.VMEM((rank, rank), jnp.float32)],
        cost_estimate=pl.CostEstimate(flops=4_000_000_000, bytes_accessed=49152, transcendentals=64),
        compiler_params=pltpu.CompilerParams(vmem_limit_bytes=VMEM_BYTES),
        name="inverse_factor",
    )(zero, one)


def scale_share(parts_ref, pair_ref, out_ref):
    rank = pair_ref.shape[0]
    share = parts_ref[0].astype(jnp.float32)
    for j in range(1, parts_ref.shape[0]):
        share = share + parts_ref[j].astype(jnp.float32)
    high = share.astype(jnp.bfloat16)
    low = (share - high.astype(jnp.float32)).astype(jnp.bfloat16)
    pair = pair_ref[...]
    scaled = contract(pair, jnp.concatenate([high, high], axis=0), ((1,), (0,)))
    scaled = scaled + contract(pair[:, :rank], low, ((1,), (0,)))
    scaled = scaled.astype(jnp.bfloat16)
    for j in range(out_ref.shape[0]):
        out_ref[j] = scaled


def scaled_copies(parts, pair, count):
    return pl.pallas_call(
        scale_share,
        out_shape=jax.ShapeDtypeStruct((count,) + parts.shape[1:], jnp.bfloat16),
        in_specs=[pl.BlockSpec(memory_space=pltpu.VMEM)] * 2,
        out_specs=pl.BlockSpec(memory_space=pltpu.VMEM),
        cost_estimate=pl.CostEstimate(flops=4_000_000, bytes_accessed=409600, transcendentals=0),
        compiler_params=pltpu.CompilerParams(vmem_limit_bytes=VMEM_BYTES),
        name="scaled_copies",
    )(parts, pair)


def on_device(grad_out, hidden, error, q_prev):
    bf16, f32 = jnp.bfloat16, jnp.float32
    g_rows, h_rows, e_rows = grad_out[0], hidden[0], error[0]
    groups, parts, plane = lax.axis_size(DP), lax.axis_size(MP), lax.axis_size(PLANE)
    rank = q_prev.shape[1]
    units = h_rows.shape[1]
    some = rank // parts

    proj_local = jnp.dot(g_rows, q_prev, preferred_element_type=f32).astype(bf16)
    first, proj_local = lax.optimization_barrier((lax.axis_index("core") == 0, proj_local))
    proj = spread(proj_local.T, MP)
    base = jnp.dot(e_rows, q_prev, preferred_element_type=f32).T
    p_terms = left_terms(proj, h_rows, base, groups)
    p_copies = sum_copies(exchange(p_terms, DP))
    parts_of_mixed, p_sum = mixed_terms(exchange(p_copies, DP), h_rows, rank, units, parts)
    got = exchange(parts_of_mixed, MP)
    mixed = total(got[:, :rank]).astype(bf16)
    gram_rows = jnp.concatenate(halves(whole(total(got[:, rank : rank + some]))), axis=1)

    q_local = contract(p_sum, e_rows, ((1,), (0,))) + contract(mixed, g_rows, ((1,), (0,)))
    half = q_local.shape[1] // 2
    left, right = q_local[:, :half], q_local[:, half:]
    other = swap(jnp.where(first, right, left).astype(bf16))
    gram_rows = jnp.pad(gram_rows, ((0, 8 - some), (0, 0)))
    q_pair = (jnp.where(first, left, right) + other.astype(f32)).astype(bf16)
    gram_rows = jnp.broadcast_to(gram_rows[None], (plane,) + gram_rows.shape)
    got = exchange(jnp.concatenate([by_lanes(q_pair, plane), gram_rows], axis=1), PLANE)
    q_share = total(got[:, :rank]).astype(bf16)
    q_share, got = lax.optimization_barrier((q_share, got))
    own_rows = got[: plane // 2, rank:]
    other_rows = swap(own_rows)
    zero_rows = jnp.where(first, own_rows, other_rows)
    one_rows = jnp.where(first, other_rows, own_rows)
    q_factors, p_factors = inverse_factor(zero_rows, one_rows, rank)
    q_copies = scaled_copies(spread(q_share, "z"), q_factors, plane)
    mine = exchange(q_copies, PLANE).transpose(1, 0, 2).reshape(rank, -1)
    other = swap(mine)
    q_factor = jnp.concatenate(
        [jnp.where(first, mine, other), jnp.where(first, other, mine)], axis=1
    ).T
    twice = jnp.concatenate([p_sum, p_sum], axis=0)
    p_factor = contract(p_factors, twice, ((1,), (0,))).astype(bf16).T
    return (p_factor, q_factor)


def solution(mesh):
    by_chip = Mesh(mesh.devices.reshape(SIZES), AXES)
    placed = (P(DP, MP, None), P(DP, None, MP), P(DP, MP, None), P())
    return jax.shard_map(
        on_device, mesh=by_chip, in_specs=placed, out_specs=(P(MP, None), P()), check_vma=False
    )
```

```python
import math

import jax
import jax.numpy as jnp
from jax import lax
from jax.experimental import pallas as pl
from jax.experimental.pallas import tpu as pltpu
from jax.sharding import Mesh
from jax.sharding import PartitionSpec as P

FF = 14336
GROUPS = 16
VMEM_BYTES = 4 << 20
LEFT_BYTES = 54 << 20
ROWS, LANES = 32, 128
AXES = ("z", "ylo", "yhi", "x", "core")
SIZES = (-1, 2, 2, 4, 2)
DP = ("z", "ylo")
MP = ("yhi", "x", "core")
PLANE = ("ylo", "yhi", "x")


def contract(left, right, dims):
    return lax.dot_general(left, right, (dims, ((), ())), preferred_element_type=jnp.float32)


def exchange(parts, axis):
    return lax.all_to_all(parts, axis, split_axis=0, concat_axis=0, tiled=True)


def spread(block, axis):
    size = lax.axis_size(axis)
    return exchange(jnp.broadcast_to(block[None], (size,) + block.shape), axis)


def swap(block):
    return lax.ppermute(block, "core", [(0, 1), (1, 0)])


def total(parts):
    return jnp.sum(parts.astype(jnp.float32), axis=0)


def halves(array):
    high = lax.reduce_precision(array, 8, 7)
    return high.astype(jnp.bfloat16), (array - high).astype(jnp.bfloat16)


def whole(pair):
    width = pair.shape[1] // 2
    return pair[:, :width] + pair[:, width:]


def by_lanes(array, count):
    return array.reshape(array.shape[0], count, -1).transpose(1, 0, 2)


def sum_kernel(parts_ref, out_ref):
    share = parts_ref[0].astype(jnp.float32)
    for j in range(1, parts_ref.shape[0]):
        share = share + parts_ref[j].astype(jnp.float32)
    share = share.astype(jnp.bfloat16)
    for j in range(out_ref.shape[0]):
        out_ref[j] = share


def sum_copies(parts):
    return pl.pallas_call(
        sum_kernel,
        out_shape=jax.ShapeDtypeStruct(parts.shape, parts.dtype),
        in_specs=[pl.BlockSpec(memory_space=pltpu.VMEM)],
        out_specs=pl.BlockSpec(memory_space=pltpu.VMEM),
        cost_estimate=pl.CostEstimate(flops=65536, bytes_accessed=262144, transcendentals=0),
        compiler_params=pltpu.CompilerParams(vmem_limit_bytes=VMEM_BYTES),
        name="sum_copies",
    )(parts)


def places(units):
    return [(r, c) for r in (0, ROWS) for c in range(0, units, LANES)]


def left_kernel(proj_ref, h_ref, base_ref, out_ref, held_ref, arrived):
    blocks = arrived.shape[0]
    rows = h_ref.shape[0] // blocks
    near = rows // LANES

    def fetch(j):
        at = pl.ds(j * rows, rows)
        return pltpu.make_async_copy(h_ref.at[at], held_ref.at[at], arrived.at[j])

    for j in range(blocks):
        fetch(j).start()
    terms = base_ref[...]
    for j in range(blocks):
        proj = jnp.concatenate([proj_ref[near * j + i] for i in range(near)], axis=1)
        fetch(j).wait()
        terms = terms + contract(proj, held_ref[j * rows : (j + 1) * rows], ((1,), (0,)))
    terms = terms.astype(jnp.bfloat16)
    used = places(terms.shape[1])
    for j, (r, c) in enumerate(used):
        out_ref[j] = terms[r : r + ROWS, c : c + LANES]
    for j in range(len(used), out_ref.shape[0]):
        out_ref[j] = jnp.zeros((ROWS, LANES), jnp.bfloat16)


def left_terms(proj, h_rows, base, count):
    return pl.pallas_call(
        left_kernel,
        out_shape=[
            jax.ShapeDtypeStruct((count, ROWS, LANES), jnp.bfloat16),
            jax.ShapeDtypeStruct(h_rows.shape, h_rows.dtype),
        ],
        in_specs=[
            pl.BlockSpec(memory_space=pltpu.VMEM),
            pl.BlockSpec(memory_space=pltpu.HBM),
            pl.BlockSpec(memory_space=pltpu.VMEM),
        ],
        out_specs=[pl.BlockSpec(memory_space=pltpu.VMEM)] * 2,
        scratch_shapes=[pltpu.SemaphoreType.DMA((4,))],
        cost_estimate=pl.CostEstimate(flops=1_000_000_000, bytes_accessed=4 << 20, transcendentals=0),
        compiler_params=pltpu.CompilerParams(vmem_limit_bytes=LEFT_BYTES),
        name="left_terms",
    )(proj, h_rows, base)


def mix_kernel(parts_ref, h_ref, out_ref, p_ref):
    for j, (r, c) in enumerate(places(p_ref.shape[1])):
        p_ref[r : r + ROWS, c : c + LANES] = parts_ref[j]
    p = p_ref[...]
    gram = contract(p, p, ((1,), (1,)))
    high = gram.astype(jnp.bfloat16).astype(jnp.float32)
    pair = jnp.concatenate([high, gram - high], axis=1)
    mixed = contract(p, h_ref[...], ((1,), (1,))).astype(jnp.bfloat16)
    count = out_ref.shape[0]
    some = pair.shape[0] // count
    fill = jnp.zeros((8 - some, LANES), jnp.float32)
    for j in range(count):
        rows = jnp.concatenate([pair[some * j : some * (j + 1)], fill], axis=0)
        block = mixed[:, j * LANES : (j + 1) * LANES]
        out_ref[j] = jnp.concatenate([block, rows.astype(jnp.bfloat16)], axis=0)


def mixed_terms(parts, h_rows, rank, units, count):
    return pl.pallas_call(
        mix_kernel,
        out_shape=[
            jax.ShapeDtypeStruct((count, rank + 8, LANES), jnp.bfloat16),
            jax.ShapeDtypeStruct((rank, units), jnp.bfloat16),
        ],
        in_specs=[pl.BlockSpec(memory_space=pltpu.VMEM)] * 2,
        out_specs=[pl.BlockSpec(memory_space=pltpu.VMEM)] * 2,
        cost_estimate=pl.CostEstimate(flops=1_000_000_000, bytes_accessed=4 << 20, transcendentals=0),
        compiler_params=pltpu.CompilerParams(vmem_limit_bytes=3 * VMEM_BYTES),
        name="mixed_terms",
    )(parts, h_rows)


def eliminate(zero_ref, one_ref, q_pair_ref, p_pair_ref, inverse_ref):
    rank = inverse_ref.shape[0]
    gram = []
    for j in range(rank // 8):
        gram += [ref[j].astype(jnp.float32)[:4] for ref in (zero_ref, one_ref)]
    gram = jnp.concatenate(gram, axis=0)
    gram = gram[:, :rank] + gram[:, rank:]
    row_at = lax.broadcasted_iota(jnp.int32, gram.shape, 0)
    column_at = lax.broadcasted_iota(jnp.int32, gram.shape, 1)
    start = jnp.concatenate([gram, (row_at == column_at).astype(jnp.float32)], axis=1)
    rows = [start[8 * b : 8 * b + 8, :] for b in range(rank // 8)]
    place = lax.broadcasted_iota(jnp.int32, (8, 1), 0)
    for k in range(0, rank, 2):
        at, inner = divmod(k, 8)
        one, two = rows[at][inner : inner + 1, :], rows[at][inner + 1 : inner + 2, :]
        pivot = jnp.broadcast_to(one[:, k : k + 1], one.shape)
        beside = jnp.broadcast_to(one[:, k + 1 : k + 2], one.shape)
        below = jnp.broadcast_to(two[:, k + 1 : k + 2], one.shape)
        scale = lax.rsqrt(pivot)
        inverse_ref[k : k + 1, :] = (one * scale)[:, rank:]
        unit = scale * scale
        ratio = beside * unit
        two = two - ratio * one
        scale = lax.rsqrt(below - ratio * beside)
        inverse_ref[k + 1 : k + 2, :] = (two * scale)[:, rank:]
        two = two * (scale * scale)
        one = one * unit - ratio * two
        for b in range(at, rank // 8):
            left = rows[b] - rows[b][:, k : k + 1] * one - rows[b][:, k + 1 : k + 2] * two
            rows[b] = jnp.where(place > inner + 1, left, rows[b]) if b == at else left
    inverse = inverse_ref[...]
    q_pair_ref[...] = halves_in(inverse * (1.0 / GROUPS))
    p_pair_ref[...] = halves_in(inverse * math.sqrt(FF))


def halves_in(array):
    high = array.astype(jnp.bfloat16)
    low = (array - high.astype(jnp.float32)).astype(jnp.bfloat16)
    return jnp.concatenate([high, low], axis=1)


def inverse_factor(zero, one, rank):
    pair = jax.ShapeDtypeStruct((rank, 2 * rank), jnp.bfloat16)
    return pl.pallas_call(
        eliminate,
        out_shape=[pair, pair],
        in_specs=[pl.BlockSpec(memory_space=pltpu.VMEM)] * 2,
        out_specs=[pl.BlockSpec(memory_space=pltpu.VMEM)] * 2,
        scratch_shapes=[pltpu.VMEM((rank, rank), jnp.float32)],
        cost_estimate=pl.CostEstimate(flops=4_000_000_000, bytes_accessed=49152, transcendentals=64),
        compiler_params=pltpu.CompilerParams(vmem_limit_bytes=VMEM_BYTES),
        name="inverse_factor",
    )(zero, one)


def scale_share(parts_ref, pair_ref, out_ref):
    rank = pair_ref.shape[0]
    share = parts_ref[0].astype(jnp.float32)
    for j in range(1, parts_ref.shape[0]):
        share = share + parts_ref[j].astype(jnp.float32)
    high = share.astype(jnp.bfloat16)
    low = (share - high.astype(jnp.float32)).astype(jnp.bfloat16)
    pair = pair_ref[...]
    scaled = contract(pair, jnp.concatenate([high, high], axis=0), ((1,), (0,)))
    scaled = scaled + contract(pair[:, :rank], low, ((1,), (0,)))
    scaled = scaled.astype(jnp.bfloat16)
    for j in range(out_ref.shape[0]):
        out_ref[j] = scaled


def scaled_copies(parts, pair, count):
    return pl.pallas_call(
        scale_share,
        out_shape=jax.ShapeDtypeStruct((count,) + parts.shape[1:], jnp.bfloat16),
        in_specs=[pl.BlockSpec(memory_space=pltpu.VMEM)] * 2,
        out_specs=pl.BlockSpec(memory_space=pltpu.VMEM),
        cost_estimate=pl.CostEstimate(flops=4_000_000, bytes_accessed=409600, transcendentals=0),
        compiler_params=pltpu.CompilerParams(vmem_limit_bytes=VMEM_BYTES),
        name="scaled_copies",
    )(parts, pair)


def on_device(grad_out, hidden, error, q_prev):
    bf16, f32 = jnp.bfloat16, jnp.float32
    g_rows, h_rows, e_rows = grad_out[0], hidden[0], error[0]
    groups, parts, plane = lax.axis_size(DP), lax.axis_size(MP), lax.axis_size(PLANE)
    rank = q_prev.shape[1]
    units = h_rows.shape[1]
    some = rank // parts

    proj_local = jnp.dot(g_rows, q_prev, preferred_element_type=f32).astype(bf16)
    first, proj_local = lax.optimization_barrier((lax.axis_index("core") == 0, proj_local))
    proj = spread(proj_local.T, MP)
    base = jnp.dot(e_rows, q_prev, preferred_element_type=f32).T
    p_terms, h_held = left_terms(proj, h_rows, base, groups)
    p_copies = sum_copies(exchange(p_terms, DP))
    parts_of_mixed, p_sum = mixed_terms(exchange(p_copies, DP), h_held, rank, units, parts)
    got = exchange(parts_of_mixed, MP)
    mixed = total(got[:, :rank]).astype(bf16)
    gram_rows = jnp.concatenate(halves(whole(total(got[:, rank : rank + some]))), axis=1)

    q_local = contract(p_sum, e_rows, ((1,), (0,))) + contract(mixed, g_rows, ((1,), (0,)))
    half = q_local.shape[1] // 2
    left, right = q_local[:, :half], q_local[:, half:]
    other = swap(jnp.where(first, right, left).astype(bf16))
    gram_rows = jnp.pad(gram_rows, ((0, 8 - some), (0, 0)))
    q_pair = (jnp.where(first, left, right) + other.astype(f32)).astype(bf16)
    gram_rows = jnp.broadcast_to(gram_rows[None], (plane,) + gram_rows.shape)
    got = exchange(jnp.concatenate([by_lanes(q_pair, plane), gram_rows], axis=1), PLANE)
    q_share = total(got[:, :rank]).astype(bf16)
    q_share, got = lax.optimization_barrier((q_share, got))
    own_rows = got[: plane // 2, rank:]
    other_rows = swap(own_rows)
    zero_rows = jnp.where(first, own_rows, other_rows)
    one_rows = jnp.where(first, other_rows, own_rows)
    q_factors, p_factors = inverse_factor(zero_rows, one_rows, rank)
    q_copies = scaled_copies(spread(q_share, "z"), q_factors, plane)
    mine = exchange(q_copies, PLANE).transpose(1, 0, 2).reshape(rank, -1)
    other = swap(mine)
    q_factor = jnp.concatenate(
        [jnp.where(first, mine, other), jnp.where(first, other, mine)], axis=1
    ).T
    twice = jnp.concatenate([p_sum, p_sum], axis=0)
    p_factor = contract(p_factors, twice, ((1,), (0,))).astype(bf16).T
    return (p_factor, q_factor)


def solution(mesh):
    by_chip = Mesh(mesh.devices.reshape(SIZES), AXES)
    placed = (P(DP, MP, None), P(DP, None, MP), P(DP, MP, None), P())
    return jax.shard_map(
        on_device, mesh=by_chip, in_specs=placed, out_specs=(P(MP, None), P()), check_vma=False
    )
```

```python
import math

import jax
import jax.numpy as jnp
from jax import lax
from jax.experimental import pallas as pl
from jax.experimental.pallas import tpu as pltpu
from jax.sharding import Mesh
from jax.sharding import PartitionSpec as P

FF = 14336
GROUPS = 16
VMEM_BYTES = 4 << 20
LEFT_BYTES = 50 << 20
ROWS, LANES = 32, 128
AXES = ("z", "ylo", "yhi", "x", "core")
SIZES = (-1, 2, 2, 4, 2)
DP = ("z", "ylo")
MP = ("yhi", "x", "core")
PLANE = ("ylo", "yhi", "x")


def contract(left, right, dims):
    return lax.dot_general(left, right, (dims, ((), ())), preferred_element_type=jnp.float32)


def exchange(parts, axis):
    return lax.all_to_all(parts, axis, split_axis=0, concat_axis=0, tiled=True)


def spread(block, axis):
    size = lax.axis_size(axis)
    return exchange(jnp.broadcast_to(block[None], (size,) + block.shape), axis)


def swap(block):
    return lax.ppermute(block, "core", [(0, 1), (1, 0)])


def total(parts):
    return jnp.sum(parts.astype(jnp.float32), axis=0)


def halves(array):
    high = lax.reduce_precision(array, 8, 7)
    return high.astype(jnp.bfloat16), (array - high).astype(jnp.bfloat16)


def whole(pair):
    width = pair.shape[1] // 2
    return pair[:, :width] + pair[:, width:]


def by_lanes(array, count):
    return array.reshape(array.shape[0], count, -1).transpose(1, 0, 2)


def sum_kernel(parts_ref, out_ref):
    share = parts_ref[0].astype(jnp.float32)
    for j in range(1, parts_ref.shape[0]):
        share = share + parts_ref[j].astype(jnp.float32)
    share = share.astype(jnp.bfloat16)
    for j in range(out_ref.shape[0]):
        out_ref[j] = share


def sum_copies(parts):
    return pl.pallas_call(
        sum_kernel,
        out_shape=jax.ShapeDtypeStruct(parts.shape, parts.dtype),
        in_specs=[pl.BlockSpec(memory_space=pltpu.VMEM)],
        out_specs=pl.BlockSpec(memory_space=pltpu.VMEM),
        cost_estimate=pl.CostEstimate(flops=65536, bytes_accessed=262144, transcendentals=0),
        compiler_params=pltpu.CompilerParams(vmem_limit_bytes=VMEM_BYTES),
        name="sum_copies",
    )(parts)


def places(units):
    return [(r, c) for r in (0, ROWS) for c in range(0, units, LANES)]


def left_kernel(proj_ref, h_ref, base_ref, out_ref, held_ref, arrived):
    blocks = arrived.shape[0]
    rows = h_ref.shape[0] // blocks
    near = rows // LANES

    def fetch(j):
        at = pl.ds(j * rows, rows)
        return pltpu.make_async_copy(h_ref.at[at], held_ref.at[at], arrived.at[j])

    for j in range(blocks):
        fetch(j).start()
    terms = base_ref[...]
    for j in range(blocks):
        proj = jnp.concatenate([proj_ref[near * j + i] for i in range(near)], axis=1)
        fetch(j).wait()
        terms = terms + contract(proj, held_ref[j * rows : (j + 1) * rows], ((1,), (0,)))
    terms = terms.astype(jnp.bfloat16)
    used = places(terms.shape[1])
    for j, (r, c) in enumerate(used):
        out_ref[j] = terms[r : r + ROWS, c : c + LANES]
    for j in range(len(used), out_ref.shape[0]):
        out_ref[j] = jnp.zeros((ROWS, LANES), jnp.bfloat16)


def left_terms(proj, h_rows, base, count):
    return pl.pallas_call(
        left_kernel,
        out_shape=[
            jax.ShapeDtypeStruct((count, ROWS, LANES), jnp.bfloat16),
            jax.ShapeDtypeStruct(h_rows.shape, h_rows.dtype),
        ],
        in_specs=[
            pl.BlockSpec(memory_space=pltpu.VMEM),
            pl.BlockSpec(memory_space=pltpu.HBM),
            pl.BlockSpec(memory_space=pltpu.VMEM),
        ],
        out_specs=[pl.BlockSpec(memory_space=pltpu.VMEM)] * 2,
        scratch_shapes=[pltpu.SemaphoreType.DMA((4,))],
        cost_estimate=pl.CostEstimate(flops=1_000_000_000, bytes_accessed=4 << 20, transcendentals=0),
        compiler_params=pltpu.CompilerParams(vmem_limit_bytes=LEFT_BYTES),
        name="left_terms",
    )(proj, h_rows, base)


def mix_kernel(parts_ref, h_ref, out_ref, p_ref):
    for j, (r, c) in enumerate(places(p_ref.shape[1])):
        p_ref[r : r + ROWS, c : c + LANES] = parts_ref[j]
    p = p_ref[...]
    gram = contract(p, p, ((1,), (1,)))
    high = gram.astype(jnp.bfloat16).astype(jnp.float32)
    pair = jnp.concatenate([high, gram - high], axis=1)
    mixed = contract(p, h_ref[...], ((1,), (1,))).astype(jnp.bfloat16)
    count = out_ref.shape[0]
    some = pair.shape[0] // count
    fill = jnp.zeros((8 - some, LANES), jnp.float32)
    for j in range(count):
        rows = jnp.concatenate([pair[some * j : some * (j + 1)], fill], axis=0)
        block = mixed[:, j * LANES : (j + 1) * LANES]
        out_ref[j] = jnp.concatenate([block, rows.astype(jnp.bfloat16)], axis=0)


def mixed_terms(parts, h_rows, rank, units, count):
    return pl.pallas_call(
        mix_kernel,
        out_shape=[
            jax.ShapeDtypeStruct((count, rank + 8, LANES), jnp.bfloat16),
            jax.ShapeDtypeStruct((rank, units), jnp.bfloat16),
        ],
        in_specs=[pl.BlockSpec(memory_space=pltpu.VMEM)] * 2,
        out_specs=[pl.BlockSpec(memory_space=pltpu.VMEM)] * 2,
        cost_estimate=pl.CostEstimate(flops=1_000_000_000, bytes_accessed=4 << 20, transcendentals=0),
        compiler_params=pltpu.CompilerParams(vmem_limit_bytes=3 * VMEM_BYTES),
        name="mixed_terms",
    )(parts, h_rows)


def eliminate(zero_ref, one_ref, q_pair_ref, p_pair_ref, inverse_ref):
    rank = inverse_ref.shape[0]
    gram = []
    for j in range(rank // 8):
        gram += [ref[j].astype(jnp.float32)[:4] for ref in (zero_ref, one_ref)]
    gram = jnp.concatenate(gram, axis=0)
    gram = gram[:, :rank] + gram[:, rank:]
    row_at = lax.broadcasted_iota(jnp.int32, gram.shape, 0)
    column_at = lax.broadcasted_iota(jnp.int32, gram.shape, 1)
    start = jnp.concatenate([gram, (row_at == column_at).astype(jnp.float32)], axis=1)
    rows = [start[8 * b : 8 * b + 8, :] for b in range(rank // 8)]
    place = lax.broadcasted_iota(jnp.int32, (8, 1), 0)
    for k in range(0, rank, 2):
        at, inner = divmod(k, 8)
        one, two = rows[at][inner : inner + 1, :], rows[at][inner + 1 : inner + 2, :]
        pivot = jnp.broadcast_to(one[:, k : k + 1], one.shape)
        beside = jnp.broadcast_to(one[:, k + 1 : k + 2], one.shape)
        below = jnp.broadcast_to(two[:, k + 1 : k + 2], one.shape)
        scale = lax.rsqrt(pivot)
        inverse_ref[k : k + 1, :] = (one * scale)[:, rank:]
        unit = scale * scale
        ratio = beside * unit
        two = two - ratio * one
        scale = lax.rsqrt(below - ratio * beside)
        inverse_ref[k + 1 : k + 2, :] = (two * scale)[:, rank:]
        two = two * (scale * scale)
        one = one * unit - ratio * two
        for b in range(at, rank // 8):
            left = rows[b] - rows[b][:, k : k + 1] * one - rows[b][:, k + 1 : k + 2] * two
            rows[b] = jnp.where(place > inner + 1, left, rows[b]) if b == at else left
    inverse = inverse_ref[...]
    q_pair_ref[...] = halves_in(inverse * (1.0 / GROUPS))
    p_pair_ref[...] = halves_in(inverse * math.sqrt(FF))


def halves_in(array):
    high = array.astype(jnp.bfloat16)
    low = (array - high.astype(jnp.float32)).astype(jnp.bfloat16)
    return jnp.concatenate([high, low], axis=1)


def inverse_factor(zero, one, rank):
    pair = jax.ShapeDtypeStruct((rank, 2 * rank), jnp.bfloat16)
    return pl.pallas_call(
        eliminate,
        out_shape=[pair, pair],
        in_specs=[pl.BlockSpec(memory_space=pltpu.VMEM)] * 2,
        out_specs=[pl.BlockSpec(memory_space=pltpu.VMEM)] * 2,
        scratch_shapes=[pltpu.VMEM((rank, rank), jnp.float32)],
        cost_estimate=pl.CostEstimate(flops=4_000_000_000, bytes_accessed=49152, transcendentals=64),
        compiler_params=pltpu.CompilerParams(vmem_limit_bytes=VMEM_BYTES),
        name="inverse_factor",
    )(zero, one)


def scale_share(parts_ref, pair_ref, out_ref):
    rank = pair_ref.shape[0]
    share = parts_ref[0].astype(jnp.float32)
    for j in range(1, parts_ref.shape[0]):
        share = share + parts_ref[j].astype(jnp.float32)
    high = share.astype(jnp.bfloat16)
    low = (share - high.astype(jnp.float32)).astype(jnp.bfloat16)
    pair = pair_ref[...]
    scaled = contract(pair, jnp.concatenate([high, high], axis=0), ((1,), (0,)))
    scaled = scaled + contract(pair[:, :rank], low, ((1,), (0,)))
    scaled = scaled.astype(jnp.bfloat16)
    for j in range(out_ref.shape[0]):
        out_ref[j] = scaled


def scaled_copies(parts, pair, count):
    return pl.pallas_call(
        scale_share,
        out_shape=jax.ShapeDtypeStruct((count,) + parts.shape[1:], jnp.bfloat16),
        in_specs=[pl.BlockSpec(memory_space=pltpu.VMEM)] * 2,
        out_specs=pl.BlockSpec(memory_space=pltpu.VMEM),
        cost_estimate=pl.CostEstimate(flops=4_000_000, bytes_accessed=409600, transcendentals=0),
        compiler_params=pltpu.CompilerParams(vmem_limit_bytes=VMEM_BYTES),
        name="scaled_copies",
    )(parts, pair)


def on_device(grad_out, hidden, error, q_prev):
    bf16, f32 = jnp.bfloat16, jnp.float32
    g_rows, h_rows, e_rows = grad_out[0], hidden[0], error[0]
    groups, parts, plane = lax.axis_size(DP), lax.axis_size(MP), lax.axis_size(PLANE)
    rank = q_prev.shape[1]
    units = h_rows.shape[1]
    some = rank // parts

    proj_local = jnp.dot(g_rows, q_prev, preferred_element_type=f32).astype(bf16)
    first, proj_local = lax.optimization_barrier((lax.axis_index("core") == 0, proj_local))
    proj = spread(proj_local.T, MP)
    base = jnp.dot(e_rows, q_prev, preferred_element_type=f32).T
    p_terms, h_held = left_terms(proj, h_rows, base, groups)
    p_copies = sum_copies(exchange(p_terms, DP))
    parts_of_mixed, p_sum = mixed_terms(exchange(p_copies, DP), h_held, rank, units, parts)
    got = exchange(parts_of_mixed, MP)
    mixed = total(got[:, :rank]).astype(bf16)
    gram_rows = jnp.concatenate(halves(whole(total(got[:, rank : rank + some]))), axis=1)

    q_local = contract(p_sum, e_rows, ((1,), (0,))) + contract(mixed, g_rows, ((1,), (0,)))
    half = q_local.shape[1] // 2
    left, right = q_local[:, :half], q_local[:, half:]
    other = swap(jnp.where(first, right, left).astype(bf16))
    gram_rows = jnp.pad(gram_rows, ((0, 8 - some), (0, 0)))
    q_pair = (jnp.where(first, left, right) + other.astype(f32)).astype(bf16)
    gram_rows = jnp.broadcast_to(gram_rows[None], (plane,) + gram_rows.shape)
    got = exchange(jnp.concatenate([by_lanes(q_pair, plane), gram_rows], axis=1), PLANE)
    q_share = total(got[:, :rank]).astype(bf16)
    q_share, got = lax.optimization_barrier((q_share, got))
    own_rows = got[: plane // 2, rank:]
    other_rows = swap(own_rows)
    zero_rows = jnp.where(first, own_rows, other_rows)
    one_rows = jnp.where(first, other_rows, own_rows)
    q_factors, p_factors = inverse_factor(zero_rows, one_rows, rank)
    q_copies = scaled_copies(spread(q_share, "z"), q_factors, plane)
    mine = exchange(q_copies, PLANE).transpose(1, 0, 2).reshape(rank, -1)
    other = swap(mine)
    q_factor = jnp.concatenate(
        [jnp.where(first, mine, other), jnp.where(first, other, mine)], axis=1
    ).T
    twice = jnp.concatenate([p_sum, p_sum], axis=0)
    p_factor = contract(p_factors, twice, ((1,), (0,))).astype(bf16).T
    return (p_factor, q_factor)


def solution(mesh):
    by_chip = Mesh(mesh.devices.reshape(SIZES), AXES)
    placed = (P(DP, MP, None), P(DP, None, MP), P(DP, MP, None), P())
    return jax.shard_map(
        on_device, mesh=by_chip, in_specs=placed, out_specs=(P(MP, None), P()), check_vma=False
    )
```

```python
import math

import jax
import jax.numpy as jnp
from jax import lax
from jax.experimental import pallas as pl
from jax.experimental.pallas import tpu as pltpu
from jax.sharding import Mesh
from jax.sharding import PartitionSpec as P

FF = 14336
GROUPS = 16
VMEM_BYTES = 4 << 20
ROWS, LANES = 32, 128
AXES = ("z", "ylo", "yhi", "x", "core")
SIZES = (-1, 2, 2, 4, 2)
DP = ("z", "ylo")
MP = ("yhi", "x", "core")
PLANE = ("ylo", "yhi", "x")


def contract(left, right, dims):
    return lax.dot_general(left, right, (dims, ((), ())), preferred_element_type=jnp.float32)


def exchange(parts, axis):
    return lax.all_to_all(parts, axis, split_axis=0, concat_axis=0, tiled=True)


def spread(block, axis):
    size = lax.axis_size(axis)
    return exchange(jnp.broadcast_to(block[None], (size,) + block.shape), axis)


def swap(block):
    return lax.ppermute(block, "core", [(0, 1), (1, 0)])


def total(parts):
    return jnp.sum(parts.astype(jnp.float32), axis=0)


def halves(array):
    high = lax.reduce_precision(array, 8, 7)
    return high.astype(jnp.bfloat16), (array - high).astype(jnp.bfloat16)


def whole(pair):
    width = pair.shape[1] // 2
    return pair[:, :width] + pair[:, width:]


def by_lanes(array, count):
    return array.reshape(array.shape[0], count, -1).transpose(1, 0, 2)


def sum_kernel(parts_ref, out_ref):
    share = parts_ref[0].astype(jnp.float32)
    for j in range(1, parts_ref.shape[0]):
        share = share + parts_ref[j].astype(jnp.float32)
    share = share.astype(jnp.bfloat16)
    for j in range(out_ref.shape[0]):
        out_ref[j] = share


def sum_copies(parts):
    return pl.pallas_call(
        sum_kernel,
        out_shape=jax.ShapeDtypeStruct(parts.shape, parts.dtype),
        in_specs=[pl.BlockSpec(memory_space=pltpu.VMEM)],
        out_specs=pl.BlockSpec(memory_space=pltpu.VMEM),
        cost_estimate=pl.CostEstimate(flops=65536, bytes_accessed=262144, transcendentals=0),
        compiler_params=pltpu.CompilerParams(vmem_limit_bytes=VMEM_BYTES),
        name="sum_copies",
    )(parts)


def places(units):
    return [(r, c) for r in (0, ROWS) for c in range(0, units, LANES)]


def hold_kernel(h_ref, held_ref):
    held_ref[...] = h_ref[...]


def hold(h_rows):
    return pl.pallas_call(
        hold_kernel,
        out_shape=jax.ShapeDtypeStruct(h_rows.shape, h_rows.dtype),
        in_specs=[pl.BlockSpec(memory_space=pltpu.VMEM)],
        out_specs=pl.BlockSpec(memory_space=pltpu.VMEM),
        cost_estimate=pl.CostEstimate(flops=0, bytes_accessed=8 << 20, transcendentals=0),
        compiler_params=pltpu.CompilerParams(vmem_limit_bytes=3 * VMEM_BYTES),
        name="hold",
    )(h_rows)


def left_kernel(proj_ref, h_ref, base_ref, out_ref):
    proj = jnp.concatenate([proj_ref[j] for j in range(proj_ref.shape[0])], axis=1)
    terms = base_ref[...] + contract(proj, h_ref[...], ((1,), (0,)))
    terms = terms.astype(jnp.bfloat16)
    used = places(terms.shape[1])
    for j, (r, c) in enumerate(used):
        out_ref[j] = terms[r : r + ROWS, c : c + LANES]
    for j in range(len(used), out_ref.shape[0]):
        out_ref[j] = jnp.zeros((ROWS, LANES), jnp.bfloat16)


def left_terms(proj, h_rows, base, count):
    return pl.pallas_call(
        left_kernel,
        out_shape=jax.ShapeDtypeStruct((count, ROWS, LANES), jnp.bfloat16),
        in_specs=[pl.BlockSpec(memory_space=pltpu.VMEM)] * 3,
        out_specs=pl.BlockSpec(memory_space=pltpu.VMEM),
        cost_estimate=pl.CostEstimate(flops=1_000_000_000, bytes_accessed=4 << 20, transcendentals=0),
        compiler_params=pltpu.CompilerParams(vmem_limit_bytes=3 * VMEM_BYTES),
        name="left_terms",
    )(proj, h_rows, base)


def mix_kernel(parts_ref, h_ref, out_ref, p_ref):
    for j, (r, c) in enumerate(places(p_ref.shape[1])):
        p_ref[r : r + ROWS, c : c + LANES] = parts_ref[j]
    p = p_ref[...]
    gram = contract(p, p, ((1,), (1,)))
    high = gram.astype(jnp.bfloat16).astype(jnp.float32)
    pair = jnp.concatenate([high, gram - high], axis=1)
    mixed = contract(p, h_ref[...], ((1,), (1,))).astype(jnp.bfloat16)
    count = out_ref.shape[0]
    some = pair.shape[0] // count
    fill = jnp.zeros((8 - some, LANES), jnp.float32)
    for j in range(count):
        rows = jnp.concatenate([pair[some * j : some * (j + 1)], fill], axis=0)
        block = mixed[:, j * LANES : (j + 1) * LANES]
        out_ref[j] = jnp.concatenate([block, rows.astype(jnp.bfloat16)], axis=0)


def mixed_terms(parts, h_rows, rank, units, count):
    return pl.pallas_call(
        mix_kernel,
        out_shape=[
            jax.ShapeDtypeStruct((count, rank + 8, LANES), jnp.bfloat16),
            jax.ShapeDtypeStruct((rank, units), jnp.bfloat16),
        ],
        in_specs=[pl.BlockSpec(memory_space=pltpu.VMEM)] * 2,
        out_specs=[pl.BlockSpec(memory_space=pltpu.VMEM)] * 2,
        cost_estimate=pl.CostEstimate(flops=1_000_000_000, bytes_accessed=4 << 20, transcendentals=0),
        compiler_params=pltpu.CompilerParams(vmem_limit_bytes=3 * VMEM_BYTES),
        name="mixed_terms",
    )(parts, h_rows)


def eliminate(zero_ref, one_ref, q_pair_ref, p_pair_ref, inverse_ref):
    rank = inverse_ref.shape[0]
    gram = []
    for j in range(rank // 8):
        gram += [ref[j].astype(jnp.float32)[:4] for ref in (zero_ref, one_ref)]
    gram = jnp.concatenate(gram, axis=0)
    gram = gram[:, :rank] + gram[:, rank:]
    row_at = lax.broadcasted_iota(jnp.int32, gram.shape, 0)
    column_at = lax.broadcasted_iota(jnp.int32, gram.shape, 1)
    start = jnp.concatenate([gram, (row_at == column_at).astype(jnp.float32)], axis=1)
    rows = [start[8 * b : 8 * b + 8, :] for b in range(rank // 8)]
    place = lax.broadcasted_iota(jnp.int32, (8, 1), 0)
    for k in range(0, rank, 2):
        at, inner = divmod(k, 8)
        one, two = rows[at][inner : inner + 1, :], rows[at][inner + 1 : inner + 2, :]
        pivot = jnp.broadcast_to(one[:, k : k + 1], one.shape)
        beside = jnp.broadcast_to(one[:, k + 1 : k + 2], one.shape)
        below = jnp.broadcast_to(two[:, k + 1 : k + 2], one.shape)
        scale = lax.rsqrt(pivot)
        inverse_ref[k : k + 1, :] = (one * scale)[:, rank:]
        unit = scale * scale
        ratio = beside * unit
        two = two - ratio * one
        scale = lax.rsqrt(below - ratio * beside)
        inverse_ref[k + 1 : k + 2, :] = (two * scale)[:, rank:]
        two = two * (scale * scale)
        one = one * unit - ratio * two
        for b in range(at, rank // 8):
            left = rows[b] - rows[b][:, k : k + 1] * one - rows[b][:, k + 1 : k + 2] * two
            rows[b] = jnp.where(place > inner + 1, left, rows[b]) if b == at else left
    inverse = inverse_ref[...]
    q_pair_ref[...] = halves_in(inverse * (1.0 / GROUPS))
    p_pair_ref[...] = halves_in(inverse * math.sqrt(FF))


def halves_in(array):
    high = array.astype(jnp.bfloat16)
    low = (array - high.astype(jnp.float32)).astype(jnp.bfloat16)
    return jnp.concatenate([high, low], axis=1)


def inverse_factor(zero, one, rank):
    pair = jax.ShapeDtypeStruct((rank, 2 * rank), jnp.bfloat16)
    return pl.pallas_call(
        eliminate,
        out_shape=[pair, pair],
        in_specs=[pl.BlockSpec(memory_space=pltpu.VMEM)] * 2,
        out_specs=[pl.BlockSpec(memory_space=pltpu.VMEM)] * 2,
        scratch_shapes=[pltpu.VMEM((rank, rank), jnp.float32)],
        cost_estimate=pl.CostEstimate(flops=4_000_000_000, bytes_accessed=49152, transcendentals=64),
        compiler_params=pltpu.CompilerParams(vmem_limit_bytes=VMEM_BYTES),
        name="inverse_factor",
    )(zero, one)


def scale_share(parts_ref, pair_ref, out_ref):
    rank = pair_ref.shape[0]
    share = parts_ref[0].astype(jnp.float32)
    for j in range(1, parts_ref.shape[0]):
        share = share + parts_ref[j].astype(jnp.float32)
    high = share.astype(jnp.bfloat16)
    low = (share - high.astype(jnp.float32)).astype(jnp.bfloat16)
    pair = pair_ref[...]
    scaled = contract(pair, jnp.concatenate([high, high], axis=0), ((1,), (0,)))
    scaled = scaled + contract(pair[:, :rank], low, ((1,), (0,)))
    scaled = scaled.astype(jnp.bfloat16)
    for j in range(out_ref.shape[0]):
        out_ref[j] = scaled


def scaled_copies(parts, pair, count):
    return pl.pallas_call(
        scale_share,
        out_shape=jax.ShapeDtypeStruct((count,) + parts.shape[1:], jnp.bfloat16),
        in_specs=[pl.BlockSpec(memory_space=pltpu.VMEM)] * 2,
        out_specs=pl.BlockSpec(memory_space=pltpu.VMEM),
        cost_estimate=pl.CostEstimate(flops=4_000_000, bytes_accessed=409600, transcendentals=0),
        compiler_params=pltpu.CompilerParams(vmem_limit_bytes=VMEM_BYTES),
        name="scaled_copies",
    )(parts, pair)


def on_device(grad_out, hidden, error, q_prev):
    bf16, f32 = jnp.bfloat16, jnp.float32
    g_rows, h_rows, e_rows = grad_out[0], hidden[0], error[0]
    groups, parts, plane = lax.axis_size(DP), lax.axis_size(MP), lax.axis_size(PLANE)
    rank = q_prev.shape[1]
    units = h_rows.shape[1]
    some = rank // parts

    proj_local = jnp.dot(g_rows, q_prev, preferred_element_type=f32).astype(bf16)
    first, proj_local = lax.optimization_barrier((lax.axis_index("core") == 0, proj_local))
    proj = spread(proj_local.T, MP)
    base = jnp.dot(e_rows, q_prev, preferred_element_type=f32).T
    base, h_rows = lax.optimization_barrier((base, h_rows))
    h_held = hold(h_rows)
    p_terms = left_terms(proj, h_held, base, groups)
    p_copies = sum_copies(exchange(p_terms, DP))
    parts_of_mixed, p_sum = mixed_terms(exchange(p_copies, DP), h_held, rank, units, parts)
    got = exchange(parts_of_mixed, MP)
    mixed = total(got[:, :rank]).astype(bf16)
    gram_rows = jnp.concatenate(halves(whole(total(got[:, rank : rank + some]))), axis=1)

    q_local = contract(p_sum, e_rows, ((1,), (0,))) + contract(mixed, g_rows, ((1,), (0,)))
    half = q_local.shape[1] // 2
    left, right = q_local[:, :half], q_local[:, half:]
    other = swap(jnp.where(first, right, left).astype(bf16))
    gram_rows = jnp.pad(gram_rows, ((0, 8 - some), (0, 0)))
    q_pair = (jnp.where(first, left, right) + other.astype(f32)).astype(bf16)
    gram_rows = jnp.broadcast_to(gram_rows[None], (plane,) + gram_rows.shape)
    got = exchange(jnp.concatenate([by_lanes(q_pair, plane), gram_rows], axis=1), PLANE)
    q_share = total(got[:, :rank]).astype(bf16)
    q_share, got = lax.optimization_barrier((q_share, got))
    own_rows = got[: plane // 2, rank:]
    other_rows = swap(own_rows)
    zero_rows = jnp.where(first, own_rows, other_rows)
    one_rows = jnp.where(first, other_rows, own_rows)
    q_factors, p_factors = inverse_factor(zero_rows, one_rows, rank)
    q_copies = scaled_copies(spread(q_share, "z"), q_factors, plane)
    mine = exchange(q_copies, PLANE).transpose(1, 0, 2).reshape(rank, -1)
    other = swap(mine)
    q_factor = jnp.concatenate(
        [jnp.where(first, mine, other), jnp.where(first, other, mine)], axis=1
    ).T
    twice = jnp.concatenate([p_sum, p_sum], axis=0)
    p_factor = contract(p_factors, twice, ((1,), (0,))).astype(bf16).T
    return (p_factor, q_factor)


def solution(mesh):
    by_chip = Mesh(mesh.devices.reshape(SIZES), AXES)
    placed = (P(DP, MP, None), P(DP, None, MP), P(DP, MP, None), P())
    return jax.shard_map(
        on_device, mesh=by_chip, in_specs=placed, out_specs=(P(MP, None), P()), check_vma=False
    )
```
